512 devices in a mesh: ctx: 128 (over x_lo, y, z), rep: 4 (over x_hi, core).
Axes of the slice: x: 4 (x_hi: 2, x_lo: 2; x = x_hi * 2 + x_lo), y: 4, z: 16, core: 2. Of those that a mesh axis runs over, the one named last changes fastest.
Arguments:
- projected: bfloat16 [3, 4096, 16384], P(None, 'rep', 'ctx'), may hold values from -6 to 6
- short_taps: float32 [3, 4096, 3], P(None, 'rep'), may hold values from -3 to 3
- residues: float32 [4096, 16], P('rep'), may hold values from -1.5 to 1.5
- decay_rates: float32 [4096, 16], P('rep'), may hold values from 0 to 1, as said below
- skip_gain: float32 [4096], P('rep'), may hold values from -4 to 4
- out_weight: bfloat16 [4096, 4096], P('ctx', 'rep'), may hold values from -0.09375 to 0.09375
Outputs:
- mixed_out: bfloat16 [4096, 16384], P('rep', 'ctx')
The draws below stay inside these ranges and needn't reach their ends.
Inputs may be any that keep to these rules, and one draw needn't show every extreme that they name: `decay_rates`: positive decay rates, none above 1/30.
All inputs are finite; a program needn't handle non-finite values.
Results may differ from the reference program's by a relative error of at most 0.015.
Values may be sent and summed in bfloat16 or wider, within the bound.
A program may use at most 128 MiB of HBM per device.

```python
import math
import jax
import jax.numpy as jnp
from jax import lax

D = 4096
K = 3
M = 16
SEQ = 16384


def draw_decay_rates(key, part):
    key = jax.random.fold_in(key, 7)
    key_slow = jax.random.fold_in(key, 0)
    slowest = math.log(0.5 / SEQ)
    fastest = math.log(1.0 / 30.0)
    return jnp.exp(jax.random.uniform(key_slow, (D, M), jnp.float32, slowest, fastest))


def steps_of(own_key, extent, shards, least, top_value):
    def one(dim, parts):
        heights = jax.random.uniform(jax.random.fold_in(jax.random.fold_in(own_key, 6), dim), (parts,), jnp.float32, least / len(shards), top_value / len(shards))
        return jnp.repeat(jnp.exp(heights), extent[dim] // parts).reshape((-1,) + (1,) * (len(extent) - dim - 1))

    loudness = one(*shards[0])
    for cut in shards[1:]:
        loudness = loudness * one(*cut)
    return loudness


def centred(rng, shape, spread, most, cuts=(), kind=jnp.bfloat16):
    result = spread * jax.random.normal(rng, shape, jnp.float32)
    if cuts:
        result = result * steps_of(rng, shape, cuts, -0.22, 0.18)
    return jnp.clip(result, -most, most).astype(kind)


def setup_inputs(seed: int = 0) -> dict:
    splits = jax.random.split(jax.random.key(seed), 7)
    return {
        "projected": centred(splits[0], (3, D, SEQ), 1.0, 6.0, ((1, 4), (2, 128))),
        "short_taps": centred(splits[1], (3, D, K), 0.6, 3.0, ((1, 4),), jnp.float32),
        "residues": centred(splits[2], (D, M), 0.25, 1.5, ((0, 4),), jnp.float32),
        "decay_rates": draw_decay_rates(jax.random.fold_in(splits[6], 71), 0),
        "skip_gain": centred(splits[4], (D,), 1.0, 4.0, ((0, 4),), jnp.float32),
        "out_weight": centred(splits[5], (D, D), D ** -0.5, 0.09375, ((0, 128), (1, 4))),
    }


def featurize(projected, short_taps):
    tap_count = short_taps.shape[2]
    length = projected.shape[2]
    widened = jnp.pad(projected.astype(jnp.float32), ((0, 0), (0, 0), (tap_count - 1, 0)))
    running = short_taps[:, :, 0:1] * widened[:, :, tap_count - 1:]
    for offset in range(1, tap_count):
        begin = tap_count - 1 - offset
        running = running + short_taps[:, :, offset:offset + 1] * widened[:, :, begin:begin + length]
    return running

def long_block(block):
    product, residues, rates, skip = block
    positions = jnp.arange(SEQ).astype(jnp.float32)
    impulse = jnp.zeros(product.shape, jnp.float32)
    for mode_index in range(M):
        weighting = residues[:, mode_index] * jnp.sqrt(2.0 * rates[:, mode_index])
        impulse = impulse + weighting[:, None] * jnp.exp(-rates[:, mode_index][:, None] * positions)
    signal = product.astype(jnp.float32)
    spectrum = jnp.fft.rfft(signal, n=2 * SEQ) * jnp.fft.rfft(impulse, n=2 * SEQ)
    convolved = jnp.fft.irfft(spectrum, n=2 * SEQ)[:, :SEQ]
    return (convolved + skip[:, None] * signal).astype(jnp.bfloat16)

def reference(projected, short_taps, residues, decay_rates, skip_gain, out_weight):
    featured = featurize(projected, short_taps)
    gate_stream = featured[0].astype(jnp.bfloat16)
    product = (featured[1] * featured[2]).astype(jnp.bfloat16)
    block_rows = min(D, 256)
    block_count = D // block_rows
    mixed_long = lax.map(long_block, (product.reshape(block_count, block_rows, SEQ), residues.reshape(block_count, block_rows, M), decay_rates.reshape(block_count, block_rows, M), skip_gain.reshape(block_count, block_rows)))
    mixed_long = mixed_long.reshape(D, SEQ)
    gated = (gate_stream.astype(jnp.float32) * mixed_long.astype(jnp.float32)).astype(jnp.bfloat16)
    return jnp.dot(out_weight.T, gated, preferred_element_type=jnp.float32).astype(jnp.bfloat16)
```

```python
import math

import numpy as np
import jax
import jax.numpy as jnp
from jax import lax
from jax.experimental import pallas as pl
from jax.experimental.pallas import tpu as pltpu
from jax.sharding import PartitionSpec as P

X, Y, Z = 2, 4, 16
REPS = 4
MODES = 16
KC = 256
F32 = jnp.float32
BF16 = jnp.bfloat16
EXACT = lax.Precision.HIGHEST


def tables(length):
    k = np.arange(length)[:, None]
    t = np.arange(length)[None, :]
    angle = math.pi * ((2 * k + 1) * t % (4 * length)) / (2 * length)
    forward = np.concatenate([np.cos(angle), -np.sin(angle)], axis=0)
    return forward.astype(np.float32), (forward.T / length).astype(np.float32)


def kernel(
    proj, par, rates3, amps3, rate_tiles, fwd, bwd, w_shard, out,
    xs, halo_s, halo_r, prod, gate, spec, local, s_send, s_recv, t_send, t_recv, p_send, p_recv,
    gall, wg, acc, o_send, o_recv,
    halo_sem, s_ssem, s_rsem, t_ssem, t_rsem, p_ssem, p_rsem,
    w_rsem, wx_ssem, wy_ssem, wz_ssem, g_rsem, g_ssem, f_ssem, h_ssem, o_sem,
):
    chans, length = proj.shape[1], proj.shape[2]
    groups = chans // 128
    rows = w_shard.shape[0]
    half = w_shard.shape[1] // 2
    pieces = chans // KC
    steps = length // 8

    ctx = lax.axis_index("ctx")
    rep = lax.axis_index("rep")
    z = lax.rem(ctx, Z)
    y = lax.rem(ctx // Z, Y)
    xl = ctx // (Y * Z)
    xo = 1 - xl
    line = ctx // Z
    rep_core = rep + 1 - 2 * lax.rem(rep, 2)
    rep_far = rep + 2 - 4 * (rep // 2)

    def at(x_, y_, z_):
        return (x_ * Y + y_) * Z + z_

    def remote(src, dst, ssem, rsem, c, r=None):
        return pltpu.make_async_remote_copy(
            src_ref=src, dst_ref=dst, send_sem=ssem, recv_sem=rsem,
            device_id=(c, rep if r is None else r), device_id_type=pl.DeviceIdType.MESH,
        )

    nxt = lax.rem(ctx + 1, X * Y * Z)
    prv = lax.rem(ctx + X * Y * Z - 1, X * Y * Z)
    zr = at(xl, y, lax.rem(z + 1, Z))
    zl = at(xl, y, lax.rem(z + Z - 1, Z))

    bar = pltpu.get_barrier_semaphore()

    def hello(c, r):
        pl.semaphore_signal(bar, inc=1, device_id=(c, r), device_id_type=pl.DeviceIdType.MESH)

    hello(nxt, rep)
    hello(prv, rep)

    @pl.loop(1, Z)
    def _(d):
        hello(at(xl, y, lax.rem(z + d, Z)), rep)

    @pl.loop(1, X * Y)
    def _(d):
        hello(lax.rem(line + d, X * Y) * Z + z, rep)

    cx = at(xo, y, z)
    hello(ctx, rep_core)
    hello(cx, rep_far)
    pl.semaphore_wait(bar, 2 + (Z - 1) + (X * Y - 1) + 2)

    def wrow(b):
        return wg.at[pl.ds(pl.multiple_of(b * rows, rows), rows), :]

    def wblock(b, ssem, c):
        return remote(wrow(b), wrow(b), ssem, w_rsem.at[b], c)

    def wcols(i):
        return w_shard.at[:, pl.ds(pl.multiple_of(i * half, half), half)]

    other = ctx + (1 - 2 * xl) * (Y * Z)
    x_copy = remote(wcols(xo), wrow(ctx), wx_ssem.at[0], w_rsem.at[ctx], cx)
    x_copy.start()
    own = pltpu.make_async_copy(wcols(xl), wrow(ctx), wx_ssem.at[1])
    own.start()

    def a_blk(d_y, d_z):
        return at(0, lax.rem(y + d_y, Y), lax.rem(z + d_z + Z, Z))

    def b_blk(d_y, d_z):
        return at(1, lax.rem(y + d_y, Y), lax.rem(z + d_z + Z, Z))

    def peer_y(d):
        return at(xl, lax.rem(y + d, Y), z)

    def w_arrived(b):
        wblock(b, wx_ssem.at[0], ctx).wait_recv()

    def a_spread(d_z):
        b = a_blk(0, d_z)
        for j in range(1, Y):
            wblock(b, wy_ssem.at[(j - 1) * Z + lax.rem(d_z + Z, Z)], peer_y(j)).start()

    RZ = Z // 2

    def zs(part, right, k):
        return wz_ssem.at[(part * 2 + right) * RZ + k]

    def a_start():
        wblock(a_blk(0, 0), zs(0, 1, 0), zr).start()
        wblock(a_blk(0, 0), zs(0, 0, 0), zl).start()
        a_spread(0)

    def a_step(k):
        w_arrived(a_blk(0, -k))
        wblock(a_blk(0, -k), zs(0, 1, k), zr).start()
        a_spread(-k)
        w_arrived(a_blk(0, k))

        @pl.when(k < RZ - 1)
        def _():
            wblock(a_blk(0, k), zs(0, 0, k), zl).start()

        a_spread(k)

    def a_last():
        w_arrived(a_blk(0, -RZ))
        a_spread(-RZ)

    def b_begin():
        for j in range(1, Y):
            wblock(b_blk(0, 0), wy_ssem.at[(Y - 1) * Z + j - 1], peer_y(j)).start()

    def b_start():
        for j in range(Y):
            if j:
                w_arrived(b_blk(j, 0))
            wblock(b_blk(j, 0), zs(1 + j, 1, 0), zr).start()
            wblock(b_blk(j, 0), zs(1 + j, 0, 0), zl).start()

    def b_step(k):
        for j in range(Y):
            w_arrived(b_blk(j, -k))
            w_arrived(b_blk(j, k))
            right = (lambda j=j: wblock(b_blk(j, -k), zs(1 + j, 1, k), zr).start())
            left = (lambda j=j: wblock(b_blk(j, k), zs(1 + j, 0, k), zl).start())
            if j < Y // 2:
                right()
                pl.when(k < RZ - 1)(left)
            else:
                pl.when(k < RZ - 1)(right)
                left()

    def b_last():
        for j in range(Y):
            w_arrived(b_blk(j, RZ))

    def w_step(k):
        if k < RZ:
            a_step(k)
            b_step(k)

    eye = (
        lax.broadcasted_iota(jnp.int32, (length, length), 0)
        == lax.broadcasted_iota(jnp.int32, (length, length), 1)
    ).astype(BF16)

    def lanes(g, width=128):
        return pl.ds(pl.multiple_of(g * width, width), width)

    @pl.loop(0, groups)
    def _(g):
        for s in range(3):
            xs[s, pl.ds(8, length), lanes(g)] = lax.dot_general(
                eye, proj[s, lanes(g), :], (((1,), (1,)), ((), ())), preferred_element_type=F32
            )

    halo_s[...] = jnp.zeros_like(halo_s)
    for s in range(3):
        halo_s[pl.ds(2 * s, 2), :] = xs[s, pl.ds(8 + length - 2, 2), :]
    halo = remote(halo_s, halo_r, halo_sem.at[0], halo_sem.at[1], nxt)
    halo.start()

    own.wait()
    w_arrived(other)
    a_start()
    b_begin()

    sub = lax.broadcasted_iota(jnp.int32, (MODES, 8, 128), 1).astype(F32)

    @pl.loop(0, groups)
    def _(g):
        r = rates3[:, :, lanes(g)]
        w = amps3[:, :, lanes(g)] * jnp.sqrt(2.0 * r)
        q = w * jnp.exp(-r * sub)
        ratio = jnp.exp(-8.0 * r)
        for a in range(steps):
            local[pl.ds(8 * a, 8), lanes(g)] = jnp.sum(q, axis=0)
            q = q * ratio

    @pl.loop(0, groups)
    def _(g):
        spec[:, lanes(g)] = jnp.dot(
            fwd[...], local[:, lanes(g)], precision=EXACT, preferred_element_type=F32
        )

    b_start()

    halo.wait_recv()
    keep = jnp.where(ctx > 0, 1.0, 0.0).astype(F32)
    for s in range(3):
        xs[s, pl.ds(6, 2), :] = halo_r[pl.ds(2 * s, 2), :] * keep

    @pl.loop(0, groups)
    def _(g):
        made = []
        for s in range(3):
            total = par[pl.ds(3 * s, 1), lanes(g)] * xs[s, pl.ds(8, length), lanes(g)]
            for j in range(1, 3):
                total = total + (
                    par[pl.ds(3 * s + j, 1), lanes(g)] * xs[s, pl.ds(8 - j, length), lanes(g)]
                )
            made.append(total)
        gate[:, lanes(g)] = made[0].astype(BF16).astype(F32)
        prod[:, lanes(g)] = (made[1] * made[2]).astype(BF16).astype(F32)
        r = rates3[:, :, lanes(g)]
        ratio = jnp.exp(-8.0 * r)
        state = jnp.zeros((MODES, 8, 128), F32)
        for a in range(steps):
            state = state * ratio + prod[pl.ds(8 * a, 8), lanes(g)][None]
        ends = jnp.sum(state * jnp.exp(-r * (7.0 - sub)), axis=1)
        s_send[g] = ends[0:8]
        s_send[groups + g] = ends[8:16]

    s_recv[z] = s_send[z]

    @pl.loop(1, Z)
    def _(d):
        to = lax.rem(z + d, Z)
        remote(s_send.at[to], s_recv.at[z], s_ssem.at[d], s_rsem.at[z], at(xl, y, to)).start()

    w_step(1)

    @pl.loop(0, groups)
    def _(g):
        u = prod[:, lanes(g)]
        u_spec = jnp.dot(fwd[...], u, precision=EXACT, preferred_element_type=F32)
        h_spec = spec[:, lanes(g)]
        u_re, u_im = u_spec[:length], u_spec[length:]
        h_re, h_im = h_spec[:length], h_spec[length:]
        joint = jnp.concatenate(
            [u_re * h_re - u_im * h_im, u_re * h_im + u_im * h_re], axis=0
        )
        mixed = jnp.dot(bwd[...], joint, precision=EXACT, preferred_element_type=F32)
        local[:, lanes(g)] = mixed + par[pl.ds(9, 1), lanes(g)] * u

    @pl.loop(1, Z)
    def _(d):
        src = lax.rem(z + d, Z)
        remote(s_send.at[z], s_recv.at[src], s_ssem.at[d], s_rsem.at[src], ctx).wait_recv()

    tile_rate = rate_tiles[z]
    block_decay = jnp.exp(-float(length) * tile_rate)
    total = jnp.zeros((8, 128), F32)
    for i in range(Z):
        total = total * block_decay + s_recv[i]
    t_send[...] = total
    t_recv[line] = total

    @pl.loop(1, X * Y)
    def _(d):
        to = lax.rem(line + d, X * Y) * Z + z
        remote(t_send, t_recv.at[line], t_ssem.at[d], t_rsem.at[line], to).start()

    w_step(2)

    @pl.loop(1, X * Y)
    def _(d):
        src = lax.rem(line + d, X * Y)
        remote(t_send, t_recv.at[src], t_ssem.at[d], t_rsem.at[src], ctx).wait_recv()

    line_decay = jnp.exp(-float(length * Z) * tile_rate)
    carry = jnp.zeros((8, 128), F32)
    for i in range(X * Y):
        carry = jnp.where(i < line, carry * line_decay + t_recv[i], carry)
    for i in range(Z):
        p_send[i] = carry
        carry = carry * block_decay + s_recv[i]
    p_recv[z] = p_send[z]

    @pl.loop(1, Z)
    def _(d):
        to = lax.rem(z + d, Z)
        remote(p_send.at[to], p_recv.at[z], p_ssem.at[d], p_rsem.at[z], at(xl, y, to)).start()

    w_step(3)

    @pl.loop(1, Z)
    def _(d):
        src = lax.rem(z + d, Z)
        remote(p_send.at[z], p_recv.at[src], p_ssem.at[d], p_rsem.at[src], ctx).wait_recv()

    def piece(x_, r_, k):
        return gall.at[x_, r_, k]

    def g_copy(x_, r_, k, ssem, c, r):
        return remote(
            piece(x_, r_, k), piece(x_, r_, k), ssem, g_rsem.at[(x_ * REPS + r_) * pieces + k], c, r
        )

    def g_arrived(x_, r_, k):
        g_copy(x_, r_, k, g_ssem.at[0], ctx, rep).wait_recv()

    per = KC // 128

    def finish(k):
        for i in range(per):
            g = k * per + i
            r = rates3[:, :, lanes(g)]
            w = amps3[:, :, lanes(g)] * jnp.sqrt(2.0 * r)
            before = jnp.concatenate([p_recv[g], p_recv[groups + g]], axis=0)
            q = (w * jnp.exp(-r * (sub + 1.0))) * before[:, None, :]
            ratio = jnp.exp(-8.0 * r)
            for a in range(steps):
                here = (pl.ds(8 * a, 8), lanes(g))
                local[here] = local[here] + jnp.sum(q, axis=0)
                q = q * ratio
            long = local[:, lanes(g)].astype(BF16).astype(F32)
            gall[xl, rep, k, :, pl.ds(128 * i, 128)] = (gate[:, lanes(g)] * long).astype(BF16)

    @pl.loop(0, pieces)
    def _(k):
        finish(k)
        g_copy(xl, rep, k, g_ssem.at[3 * k], ctx, rep_core).start()
        g_copy(xl, rep, k, g_ssem.at[3 * k + 1], cx, rep).start()
        g_copy(xl, rep, k, g_ssem.at[3 * k + 2], cx, rep_far).start()

    @pl.loop(4, RZ)
    def _(k):
        a_step(k)
        b_step(k)

    a_last()
    b_last()

    @pl.loop(0, pieces)
    def _(k):
        g_arrived(xo, rep, k)

        @pl.when(lax.rem(k, 2) == 0)
        def _():
            g_copy(xo, rep, k, h_ssem.at[k], cx, rep_far).start()

        g_copy(xo, rep, k, f_ssem.at[3 * k], ctx, rep_core).start()
        g_arrived(xo, rep_far, k)

        @pl.when(lax.rem(k, 2) == 1)
        def _():
            g_copy(xo, rep_far, k, h_ssem.at[k], cx, rep).start()

        g_copy(xo, rep_far, k, f_ssem.at[3 * k + 1], ctx, rep_core).start()

    @pl.loop(0, pieces)
    def _(k):
        g_arrived(xl, rep_far, k)
        g_copy(xl, rep_far, k, f_ssem.at[3 * k + 2], ctx, rep_core).start()

    @pl.loop(0, Z)
    def _(d):
        for j in range(1, Y):
            w_arrived(a_blk(j, d))

    acc[...] = jnp.zeros_like(acc)

    def project(r_, k):
        c0 = (r_ * pieces + k) * KC
        w_part = wg[pl.ds(pl.multiple_of(c0, KC), KC), :]
        for x_ in range(X):
            acc[pl.ds(x_ * length, length), :] += jnp.dot(
                gall[x_, r_, k], w_part, preferred_element_type=F32
            )

    @pl.loop(0, pieces)
    def _(k):
        project(rep, k)

    @pl.loop(0, pieces)
    def _(k):
        project(rep_far, k)

    for src_rep in (rep_core, rep_far + rep_core - rep):
        @pl.loop(0, pieces)
        def _(k):
            g_arrived(xl, src_rep, k)
            g_arrived(xo, src_rep, k)
            project(src_rep, k)

    o_send[...] = acc[pl.ds(pl.multiple_of(xo * length, length), length), :].astype(BF16)
    swap = remote(o_send, o_recv, o_sem.at[0], o_sem.at[1], cx)
    swap.start()
    out[xl] = acc[pl.ds(pl.multiple_of(xl * length, length), length), :].astype(BF16)

    halo.wait_send()
    x_copy.wait_send()

    @pl.loop(1, Z)
    def _(d):
        remote(s_send.at[0], s_recv.at[0], s_ssem.at[d], s_rsem.at[0], ctx).wait_send()
        remote(p_send.at[0], p_recv.at[0], p_ssem.at[d], p_rsem.at[0], ctx).wait_send()

    @pl.loop(1, X * Y)
    def _(d):
        remote(t_send, t_recv.at[0], t_ssem.at[d], t_rsem.at[0], ctx).wait_send()

    @pl.loop(0, (Y - 1) * (Z + 1))
    def _(i):
        wblock(0, wy_ssem.at[i], ctx).wait_send()

    for part in range(1 + Y):
        for right in range(2):
            full = right == (1 if part <= Y // 2 else 0)

            @pl.loop(0, RZ if full else RZ - 1)
            def _(k):
                wblock(0, zs(part, right, k), ctx).wait_send()

    @pl.loop(0, 3 * pieces)
    def _(i):
        g_copy(0, 0, 0, g_ssem.at[i], ctx, rep).wait_send()
        g_copy(0, 0, 0, f_ssem.at[i], ctx, rep).wait_send()

    @pl.loop(0, pieces)
    def _(i):
        g_copy(0, 0, 0, h_ssem.at[i], ctx, rep).wait_send()

    swap.wait()
    out[xo] = o_recv[...]


def per_device(projected, short_taps, residues, decay_rates, skip_gain, out_weight):
    _, chans, length = projected.shape
    groups = chans // 128
    rows, feats = out_weight.shape
    half = feats // X
    pieces = chans // KC
    par = jnp.concatenate(
        [
            short_taps.transpose(0, 2, 1).reshape(9, chans),
            skip_gain[None],
            jnp.zeros((6, chans), F32),
        ],
        axis=0,
    )
    rates_t = decay_rates.T
    rate_tiles = rates_t.reshape(2, 8, groups, 128).transpose(0, 2, 1, 3).reshape(Z, 8, 128)
    fwd, bwd = tables(length)
    vm = pltpu.VMEM
    dma = pltpu.SemaphoreType.DMA
    out = pl.pallas_call(
        kernel,
        out_shape=jax.ShapeDtypeStruct((X, length, half), BF16),
        in_specs=[pl.BlockSpec(memory_space=vm)] * 8,
        out_specs=pl.BlockSpec(memory_space=vm),
        scratch_shapes=[
            vm((3, length + 8, chans), F32),
            vm((8, chans), F32),
            vm((8, chans), F32),
            vm((length, chans), F32),
            vm((length, chans), F32),
            vm((2 * length, chans), F32),
            vm((length, chans), F32),
            vm((Z, 8, 128), F32),
            vm((Z, 8, 128), F32),
            vm((8, 128), F32),
            vm((X * Y, 8, 128), F32),
            vm((Z, 8, 128), F32),
            vm((Z, 8, 128), F32),
            vm((X, REPS, pieces, length, KC), BF16),
            vm((X * Y * Z * rows, half), BF16),
            vm((X * length, half), F32),
            vm((length, half), BF16),
            vm((length, half), BF16),
            dma((2,)),
            dma((Z,)),
            dma((Z,)),
            dma((X * Y,)),
            dma((X * Y,)),
            dma((Z,)),
            dma((Z,)),
            dma((X * Y * Z,)),
            dma((2,)),
            dma(((Y - 1) * (Z + 1),)),
            dma(((1 + Y) * 2 * (Z // 2),)),
            dma((X * REPS * pieces,)),
            dma((3 * pieces,)),
            dma((3 * pieces,)),
            dma((pieces,)),
            dma((2,)),
        ],
        compiler_params=pltpu.CompilerParams(
            collective_id=0, has_side_effects=True, vmem_limit_bytes=40 * 1024 * 1024
        ),
        name="hyena",
    )(
        projected, par, rates_t[:, None, :], residues.T[:, None, :], rate_tiles,
        jnp.asarray(fwd), jnp.asarray(bwd), out_weight,
    )
    return out.transpose(0, 2, 1).reshape(feats, length)


def solution(mesh):
    in_specs = (
        P(None, "rep", "ctx"),
        P(None, "rep", None),
        P("rep", None),
        P("rep", None),
        P("rep"),
        P("ctx", "rep"),
    )
    out_specs = P("rep", "ctx")
    return jax.shard_map(
        per_device, mesh=mesh, in_specs=in_specs, out_specs=out_specs, check_vma=False
    )
```

```python
import math

import numpy as np
import jax
import jax.numpy as jnp
from jax import lax
from jax.experimental import pallas as pl
from jax.experimental.pallas import tpu as pltpu
from jax.sharding import PartitionSpec as P

X, Y, Z = 2, 4, 16
ZL = 4
REPS = 4
MODES = 16
KC = 256
F32 = jnp.float32
BF16 = jnp.bfloat16


def split(value):
    high = value.astype(BF16)
    return high, (value - high.astype(F32)).astype(BF16)


def tables(length):
    k = np.arange(length)[:, None]
    t = np.arange(length)[None, :]
    angle = math.pi * ((2 * k + 1) * t % (4 * length)) / (2 * length)
    forward = np.concatenate([np.cos(angle), -np.sin(angle)], axis=0).astype(np.float32)
    backward = (forward.T / length).astype(np.float32)

    def halves(table):
        high = table.astype(jnp.bfloat16)
        return high, (table - high.astype(np.float32)).astype(jnp.bfloat16)

    return np.concatenate(halves(forward), axis=1), np.concatenate(halves(backward), axis=0)


def kernel(
    proj_hbm, taps_hbm, amps_hbm, rates_hbm, skip, fwd, bwd, w_shard, out,
    proj, taps, amps, rates, ex, rev, first, ratio, wide, carry_w, rate_tiles,
    xs, halo_s, halo_r, prod, gate, local, s_send, s_recv, t_send, t_recv, starts, p_send, p_recv,
    gall, wg, acc, o_send, o_recv,
    word_sem, in_sem, halo_sem, s_ssem, s_rsem, t_ssem, t_rsem, p_ssem, p_rsem,
    wx_sem, wz_rsem, wz_ssem, wl_rsem, wr_rsem, wy_ssem, wh_rsem, wh_ssem, g_rsem, g_ssem, f_ssem, h_ssem, o_sem,
):
    chans, length = proj.shape[1], proj.shape[2]
    groups = chans // 128
    rows = w_shard.shape[0]
    half = w_shard.shape[1] // 2
    pieces = chans // KC
    steps = length // 8

    ctx = lax.axis_index("ctx")
    rep = lax.axis_index("rep")
    z = lax.rem(ctx, Z)
    y = lax.rem(ctx // Z, Y)
    xl = ctx // (Y * Z)
    xo = 1 - xl
    rep_core = rep + 1 - 2 * lax.rem(rep, 2)
    rep_far = rep + 2 - 4 * (rep // 2)

    def at(x_, y_, z_):
        return (x_ * Y + y_) * Z + z_

    def remote(src, dst, ssem, rsem, c, r=None):
        return pltpu.make_async_remote_copy(
            src_ref=src, dst_ref=dst, send_sem=ssem, recv_sem=rsem,
            device_id=(c, rep if r is None else r), device_id_type=pl.DeviceIdType.MESH,
        )

    nxt = lax.rem(ctx + 1, X * Y * Z)
    prv = lax.rem(ctx + X * Y * Z - 1, X * Y * Z)
    zr = at(xl, y, lax.rem(z + 1, Z))
    zl = at(xl, y, lax.rem(z + Z - 1, Z))

    bar = pltpu.get_barrier_semaphore()

    def hello(c, r):
        pl.semaphore_signal(bar, inc=1, device_id=(c, r), device_id_type=pl.DeviceIdType.MESH)

    ZH = Z // ZL
    zh = z // ZL
    plane = Y * ZL
    mine = y * ZL + lax.rem(z, ZL)
    slab = xl * ZH + zh

    def plane_peer(q):
        return at(xl, q // ZL, zh * ZL + lax.rem(q, ZL))

    def slab_peer(h):
        return at(h // ZH, y, lax.rem(h, ZH) * ZL + lax.rem(z, ZL))

    up = at(xl, y, lax.rem(z + ZL, Z))
    down = at(xl, y, lax.rem(z + Z - ZL, Z))
    cx = at(xo, y, z)

    @pl.loop(1, plane)
    def _(d):
        hello(plane_peer(lax.rem(mine + d, plane)), rep)

    for c in (nxt, prv, zr, zl, up, down, cx):
        hello(c, rep)
    hello(ctx, rep_core)
    hello(cx, rep_far)
    reads = [
        pltpu.make_async_copy(proj_hbm.at[i], proj.at[i], in_sem.at[i]) for i in range(3)
    ]
    reads += [
        pltpu.make_async_copy(rates_hbm, rates, in_sem.at[3]),
        pltpu.make_async_copy(amps_hbm, amps, in_sem.at[4]),
        pltpu.make_async_copy(taps_hbm, taps, in_sem.at[5]),
    ]
    for read in reads:
        read.start()

    def lanes(g, width=128):
        return pl.ds(pl.multiple_of(g * width, width), width)

    eye = (
        lax.broadcasted_iota(jnp.int32, (length, length), 0)
        == lax.broadcasted_iota(jnp.int32, (length, length), 1)
    ).astype(BF16)

    for s in range(3):
        reads[s].wait()

        @pl.loop(0, groups)
        def _(g):
            xs[s, pl.ds(8, length), lanes(g)] = lax.dot_general(
                eye, proj[s, lanes(g), :], (((1,), (1,)), ((), ())), preferred_element_type=F32
            )

        xs[s, pl.ds(0, 8), :] = jnp.zeros((8, chans), F32)
    halo_s[...] = jnp.zeros_like(halo_s)
    for s in range(3):
        halo_s[pl.ds(2 * s, 2), :] = xs[s, pl.ds(8 + length - 2, 2), :]

    pl.semaphore_wait(bar, (plane - 1) + 7 + 2)

    def pass_on(i):
        for c in (up, down):
            pl.semaphore_signal(
                word_sem.at[i], inc=1, device_id=(c, rep), device_id_type=pl.DeviceIdType.MESH
            )

    pass_on(0)
    halo = remote(halo_s, halo_r, halo_sem.at[0], halo_sem.at[1], nxt)
    halo.start()

    RZ = Z // 2
    half_rows = rows // 2

    def wcols(i):
        return w_shard.at[:, pl.ds(pl.multiple_of(i * half, half), half)]

    x_copy = remote(wcols(xo), wg.at[xl, y, z], wx_sem.at[0], wx_sem.at[1], cx)
    x_copy.start()
    own = pltpu.make_async_copy(wcols(xl), wg.at[xl, y, z], wx_sem.at[2])
    own.start()

    def y_of(d):
        return lax.rem(y + d, Y)

    def z_of(d):
        return lax.rem(z + d + Z, Z)

    y_next, y_prev = at(xl, y_of(1), z), at(xl, y_of(Y - 1), z)

    def w_half(d_y, d_z, i, ssem, rsem, c):
        part = wg.at[:, y_of(d_y), z_of(d_z), pl.ds(i * half_rows, half_rows)]
        return remote(part, part, ssem, rsem.at[i * Z + z_of(d_z)], c)

    def w_round(d_z, i, right, k):
        ssem = wz_ssem.at[(i * 2 + right) * RZ + k]
        return w_half(0, d_z, i, ssem, wz_rsem, zr if right else zl)

    def w_arrived(d_z, i):
        w_half(0, d_z, i, wx_sem.at[0], wz_rsem, ctx).wait_recv()

    def w_whole(d_y, d_z, ssem, rsem, c):
        part = wg.at[:, y_of(d_y), z_of(d_z)]
        return remote(part, part, ssem, rsem.at[z_of(d_z)], c)

    def w_spread(d_z):
        w_whole(0, d_z, wy_ssem.at[z_of(d_z)], wl_rsem, y_next).start()
        w_whole(0, d_z, wy_ssem.at[Z + z_of(d_z)], wr_rsem, y_prev).start()

    def w_relay(d_z):
        w_whole(Y - 1, d_z, wx_sem.at[0], wl_rsem, ctx).wait_recv()
        w_half(Y - 1, d_z, 0, wh_ssem.at[z_of(d_z)], wh_rsem, y_next).start()
        w_whole(1, d_z, wx_sem.at[0], wr_rsem, ctx).wait_recv()
        w_half(1, d_z, 1, wh_ssem.at[Z + z_of(d_z)], wh_rsem, y_prev).start()

    def w_relayed(d_z):
        for i in range(2):
            w_half(2, d_z, i, wx_sem.at[0], wh_rsem, ctx).wait_recv()

    def w_start():
        own.wait()
        x_copy.wait_recv()
        for i in range(2):
            w_round(0, i, 1, 0).start()
            w_round(0, i, 0, 0).start()
        w_spread(0)

    def w_step(k):
        if k >= RZ:
            return
        for i in range(2):
            w_arrived(-k, i)
            if k < RZ - 1 or i == 0:
                w_round(-k, i, 1, k).start()
            w_arrived(k, i)
            if k < RZ - 1 or i == 1:
                w_round(k, i, 0, k).start()
        w_spread(-k)
        w_spread(k)
        w_relay(1 - k)
        if k > 1:
            w_relay(k - 1)

    def w_last():
        for i in range(2):
            w_arrived(RZ, i)
        w_spread(RZ)
        w_relay(1 - RZ)
        if RZ > 1:
            w_relay(RZ - 1)

    sub = lax.broadcasted_iota(jnp.int32, (MODES, 8, 128), 1).astype(F32)
    for read in reads[3:]:
        read.wait()

    @pl.loop(0, groups)
    def _(g):
        r2 = rates[:, lanes(g)]
        w2 = amps[:, lanes(g)] * jnp.sqrt(2.0 * r2)
        rate_tiles[g] = r2[0:8]
        rate_tiles[groups + g] = r2[8:16]
        once = w2 * jnp.exp(-r2)
        carry_w[g] = once[0:8]
        carry_w[groups + g] = once[8:16]
        r = r2[:, None, :]
        ex[:, :, lanes(g)] = jnp.exp(-r * sub)
        back = jnp.exp(-r * (7.0 - sub))
        rev[:, :, lanes(g)] = back
        first[:, :, lanes(g)] = back * jnp.exp(-float(length - 8) * r)
        ratio[:, :, lanes(g)] = jnp.exp(-8.0 * r)
        wide[:, :, lanes(g)] = w2[:, None, :]

    w_start()

    def featured(g, begin, count):
        made = []
        for s in range(3):
            total = taps[s, pl.ds(0, 1), lanes(g)] * xs[s, pl.ds(8 + begin, count), lanes(g)]
            for j in range(1, 3):
                total = total + (
                    taps[s, pl.ds(j, 1), lanes(g)]
                    * xs[s, pl.ds(8 + begin - j, count), lanes(g)]
                )
            made.append(total)
        return made[0].astype(BF16).astype(F32), (made[1] * made[2]).astype(BF16).astype(F32)

    top = lax.broadcasted_iota(jnp.int32, (8, 128), 0) < 2

    @pl.loop(0, groups)
    def _(g):
        gate_here, prod_here = featured(g, 0, length)
        gate[:, lanes(g)] = gate_here
        prod[:, lanes(g)] = prod_here
        step = ratio[:, :, lanes(g)]
        state = jnp.where(top, 0.0, prod[pl.ds(0, 8), lanes(g)])[None] * step
        for a in range(1, steps):
            state = state + prod[pl.ds(8 * a, 8), lanes(g)][None]
            if a < steps - 1:
                state = state * step
        ends = jnp.sum(state * rev[:, :, lanes(g)], axis=1)
        s_send[g] = ends[0:8]
        s_send[groups + g] = ends[8:16]

    halo.wait_recv()
    keep = jnp.where(ctx > 0, 1.0, 0.0).astype(F32)
    for s in range(3):
        xs[s, pl.ds(6, 2), :] = halo_r[pl.ds(2 * s, 2), :] * keep

    @pl.loop(0, groups)
    def _(g):
        gate_here, prod_here = featured(g, 0, 8)
        gate[pl.ds(0, 8), lanes(g)] = gate_here
        prod[pl.ds(0, 8), lanes(g)] = prod_here
        more = jnp.sum(
            first[:, :, lanes(g)] * jnp.where(top, prod_here, 0.0)[None], axis=1
        )
        s_send[g] += more[0:8]
        s_send[groups + g] += more[8:16]

    pl.semaphore_wait(word_sem.at[0], 2)
    pass_on(1)
    s_recv[mine] = s_send[mine]

    @pl.loop(1, plane)
    def _(d):
        to = lax.rem(mine + d, plane)
        remote(
            s_send.at[to], s_recv.at[mine], s_ssem.at[d], s_rsem.at[mine], plane_peer(to)
        ).start()

    w_step(1)

    @pl.loop(0, groups)
    def _(g):
        q = wide[:, :, lanes(g)] * ex[:, :, lanes(g)]
        step = ratio[:, :, lanes(g)]
        for a in range(steps):
            local[pl.ds(8 * a, 8), lanes(g)] = jnp.sum(q, axis=0)
            q = q * step

    def dot(left, right):
        return jnp.dot(left, right, preferred_element_type=F32)

    @pl.loop(0, chans // 256)
    def _(g):
        h_hi, h_lo = split(local[:, lanes(g, 256)])
        h_spec = dot(fwd[...], jnp.concatenate([h_hi, h_hi], axis=0)) + dot(fwd[:, :length], h_lo)
        u = prod[:, lanes(g, 256)]
        u_hi = u.astype(BF16)
        u_spec = dot(fwd[...], jnp.concatenate([u_hi, u_hi], axis=0))
        u_re, u_im = u_spec[:length], u_spec[length:]
        h_re, h_im = h_spec[:length], h_spec[length:]
        joint = jnp.concatenate(
            [u_re * h_re - u_im * h_im, u_re * h_im + u_im * h_re], axis=0
        )
        j_hi, j_lo = split(joint)
        mixed = dot(bwd[...], j_hi)
        mixed = mixed[:length] + mixed[length:] + dot(bwd[:length, :], j_lo)
        local[:, lanes(g, 256)] = mixed + skip[:, lanes(g, 256)] * u

    w_step(2)

    @pl.loop(1, plane)
    def _(d):
        src = lax.rem(mine + d, plane)
        remote(s_send.at[mine], s_recv.at[src], s_ssem.at[d], s_rsem.at[src], ctx).wait_recv()

    tile_rate = rate_tiles[mine]
    block_decay = jnp.exp(-float(length) * tile_rate)
    for i in range(Y):
        total = jnp.zeros((8, 128), F32)
        for j in range(ZL):
            total = total * block_decay + s_recv[i * ZL + j]
        t_send[i] = total
        t_recv[slab, i] = total
    pl.semaphore_wait(word_sem.at[1], 2)

    @pl.loop(1, X * ZH)
    def _(d):
        to = slab_peer(lax.rem(slab + d, X * ZH))
        remote(t_send, t_recv.at[slab], t_ssem.at[d], t_rsem.at[slab], to).start()

    w_step(3)
    w_step(4)

    @pl.loop(1, X * ZH)
    def _(d):
        src = lax.rem(slab + d, X * ZH)
        remote(t_send, t_recv.at[src], t_ssem.at[d], t_rsem.at[src], ctx).wait_recv()

    group_decay = jnp.exp(-float(length * ZL) * tile_rate)
    carry = jnp.zeros((8, 128), F32)
    for i in range(X):
        for j in range(Y):
            for k in range(ZH):
                starts[(i * Y + j) * ZH + k] = carry
                carry = carry * group_decay + t_recv[i * ZH + k, j]
    for i in range(Y):
        carry = starts[(xl * Y + i) * ZH + zh]
        for j in range(ZL):
            p_send[i * ZL + j] = carry
            carry = carry * block_decay + s_recv[i * ZL + j]
    p_recv[mine] = p_send[mine]

    @pl.loop(1, plane)
    def _(d):
        to = lax.rem(mine + d, plane)
        remote(
            p_send.at[to], p_recv.at[mine], p_ssem.at[d], p_rsem.at[mine], plane_peer(to)
        ).start()

    w_step(5)
    w_step(6)

    @pl.loop(1, plane)
    def _(d):
        src = lax.rem(mine + d, plane)
        remote(p_send.at[mine], p_recv.at[src], p_ssem.at[d], p_rsem.at[src], ctx).wait_recv()

    def piece(x_, r_, k):
        return gall.at[r_, k, pl.ds(pl.multiple_of(x_ * length, length), length), :]

    def g_copy(x_, r_, k, ssem, c, r):
        return remote(
            piece(x_, r_, k), piece(x_, r_, k), ssem, g_rsem.at[(x_ * REPS + r_) * pieces + k], c, r
        )

    def g_arrived(x_, r_, k):
        g_copy(x_, r_, k, g_ssem.at[0], ctx, rep).wait_recv()

    per = KC // 128

    def finish(k):
        for i in range(per):
            g = k * per + i
            before = jnp.concatenate(
                [p_recv[g] * carry_w[g], p_recv[groups + g] * carry_w[groups + g]], axis=0
            )
            q = before[:, None, :] * ex[:, :, lanes(g)]
            step = ratio[:, :, lanes(g)]
            for a in range(steps):
                here = (pl.ds(8 * a, 8), lanes(g))
                local[here] = local[here] + jnp.sum(q, axis=0)
                q = q * step
            long = local[:, lanes(g)].astype(BF16).astype(F32)
            gall[rep, k, pl.ds(pl.multiple_of(xl * length, length), length), pl.ds(128 * i, 128)] = (
                gate[:, lanes(g)] * long
            ).astype(BF16)

    @pl.loop(0, pieces)
    def _(k):
        finish(k)
        g_copy(xl, rep, k, g_ssem.at[3 * k], ctx, rep_core).start()
        g_copy(xl, rep, k, g_ssem.at[3 * k + 1], cx, rep).start()
        g_copy(xl, rep, k, g_ssem.at[3 * k + 2], cx, rep_far).start()

    def g_pass(k):
        g_arrived(xo, rep, k)
        if k % 2 == 0:
            g_copy(xo, rep, k, h_ssem.at[k], cx, rep_far).start()
        g_copy(xo, rep, k, f_ssem.at[3 * k], ctx, rep_core).start()
        g_arrived(xo, rep_far, k)
        if k % 2 == 1:
            g_copy(xo, rep_far, k, h_ssem.at[k], cx, rep).start()
        g_copy(xo, rep_far, k, f_ssem.at[3 * k + 1], ctx, rep_core).start()

    w_step(7)
    for k in range(pieces // 2):
        g_pass(k)
    w_last()
    for k in range(pieces // 2, pieces):
        g_pass(k)
    w_relay(RZ)

    @pl.loop(0, Z)
    def _(d):
        w_relayed(d)

    def project(r_, k):
        n = (r_ * pieces + k) * (KC // rows)
        part = wg[n // (Y * Z), lax.rem(n // Z, Y), pl.ds(lax.rem(n, Z), KC // rows)]
        acc[...] += jnp.dot(gall[r_, k], part.reshape(KC, half), preferred_element_type=F32)

    acc[...] = jnp.zeros_like(acc)

    @pl.loop(0, pieces)
    def _(k):
        project(rep, k)
        g_arrived(xl, rep_far, k)
        g_copy(xl, rep_far, k, f_ssem.at[3 * k + 2], ctx, rep_core).start()

    @pl.loop(0, pieces)
    def _(k):
        project(rep_far, k)

    for src_rep in (rep_core, rep_far + rep_core - rep):
        @pl.loop(0, pieces)
        def _(k):
            g_arrived(xl, src_rep, k)
            g_arrived(xo, src_rep, k)
            project(src_rep, k)

    o_send[...] = acc[pl.ds(pl.multiple_of(xo * length, length), length), :].astype(BF16)
    swap = remote(o_send, o_recv, o_sem.at[0], o_sem.at[1], cx)
    swap.start()
    out[xl] = acc[pl.ds(pl.multiple_of(xl * length, length), length), :].astype(BF16)

    halo.wait_send()
    x_copy.wait_send()

    @pl.loop(1, plane)
    def _(d):
        remote(s_send.at[0], s_recv.at[0], s_ssem.at[d], s_rsem.at[0], ctx).wait_send()
        remote(p_send.at[0], p_recv.at[0], p_ssem.at[d], p_rsem.at[0], ctx).wait_send()

    @pl.loop(1, X * ZH)
    def _(d):
        remote(t_send, t_recv.at[0], t_ssem.at[d], t_rsem.at[0], ctx).wait_send()

    @pl.loop(0, Z)
    def _(i):
        for j in range(2):
            w_whole(0, 0, wy_ssem.at[j * Z + i], wl_rsem, ctx).wait_send()
            w_half(0, 0, 0, wh_ssem.at[j * Z + i], wh_rsem, ctx).wait_send()

    for k in range(RZ):
        for i in range(2):
            for right in range(2):
                if k < RZ - 1 or i != right:
                    w_round(0, i, right, k).wait_send()

    @pl.loop(0, 3 * pieces)
    def _(i):
        g_copy(0, 0, 0, g_ssem.at[i], ctx, rep).wait_send()
        g_copy(0, 0, 0, f_ssem.at[i], ctx, rep).wait_send()

    @pl.loop(0, pieces)
    def _(i):
        g_copy(0, 0, 0, h_ssem.at[i], ctx, rep).wait_send()

    swap.wait()
    out[xo] = o_recv[...]


def per_device(projected, short_taps, residues, decay_rates, skip_gain, out_weight):
    _, chans, length = projected.shape
    groups = chans // 128
    rows, feats = out_weight.shape
    half = feats // X
    pieces = chans // KC
    fwd, bwd = tables(length)
    vm = pltpu.VMEM
    dma = pltpu.SemaphoreType.DMA
    out = pl.pallas_call(
        kernel,
        out_shape=jax.ShapeDtypeStruct((X, length, half), BF16),
        in_specs=[pl.BlockSpec(memory_space=pltpu.HBM)] * 4
        + [pl.BlockSpec(memory_space=vm)] * 3
        + [pl.BlockSpec(memory_space=pltpu.HBM)],
        out_specs=pl.BlockSpec(memory_space=vm),
        scratch_shapes=[
            vm((3, chans, length), BF16),
            vm((3, 3, chans), F32),
            vm((MODES, chans), F32),
            vm((MODES, chans), F32),
            vm((MODES, 8, chans), F32),
            vm((MODES, 8, chans), F32),
            vm((MODES, 8, chans), F32),
            vm((MODES, 1, chans), F32),
            vm((MODES, 1, chans), F32),
            vm((Y * ZL, 8, 128), F32),
            vm((Y * ZL, 8, 128), F32),
            vm((3, length + 8, chans), F32),
            vm((8, chans), F32),
            vm((8, chans), F32),
            vm((length, chans), F32),
            vm((length, chans), F32),
            vm((length, chans), F32),
            vm((Y * ZL, 8, 128), F32),
            vm((Y * ZL, 8, 128), F32),
            vm((Y, 8, 128), F32),
            vm((X * Z // ZL, Y, 8, 128), F32),
            vm((X * Y * Z // ZL, 8, 128), F32),
            vm((Y * ZL, 8, 128), F32),
            vm((Y * ZL, 8, 128), F32),
            vm((REPS, pieces, X * length, KC), BF16),
            vm((X, Y, Z, rows, half), BF16),
            vm((X * length, half), F32),
            vm((length, half), BF16),
            vm((length, half), BF16),
            pltpu.SemaphoreType.REGULAR((2,)),
            dma((6,)),
            dma((2,)),
            dma((Y * ZL,)),
            dma((Y * ZL,)),
            dma((X * Z // ZL,)),
            dma((X * Z // ZL,)),
            dma((Y * ZL,)),
            dma((Y * ZL,)),
            dma((3,)),
            dma((2 * Z,)),
            dma((2 * Z,)),
            dma((Z,)),
            dma((Z,)),
            dma((2 * Z,)),
            dma((2 * Z,)),
            dma((2 * Z,)),
            dma((X * REPS * pieces,)),
            dma((3 * pieces,)),
            dma((3 * pieces,)),
            dma((pieces,)),
            dma((2,)),
        ],
        compiler_params=pltpu.CompilerParams(
            collective_id=0, has_side_effects=True, vmem_limit_bytes=60 * 1024 * 1024
        ),
        name="hyena",
    )(
        projected, short_taps.transpose(0, 2, 1), residues.T, decay_rates.T, skip_gain[None],
        jnp.asarray(fwd), jnp.asarray(bwd), out_weight,
    )
    return out.transpose(0, 2, 1).reshape(feats, length)


def solution(mesh):
    in_specs = (
        P(None, "rep", "ctx"),
        P(None, "rep", None),
        P("rep", None),
        P("rep", None),
        P("rep"),
        P("ctx", "rep"),
    )
    out_specs = P("rep", "ctx")
    return jax.shard_map(
        per_device, mesh=mesh, in_specs=in_specs, out_specs=out_specs, check_vma=False
    )
```

```python
import math

import numpy as np
import jax
import jax.numpy as jnp
from jax import lax
from jax.experimental import pallas as pl
from jax.experimental.pallas import tpu as pltpu
from jax.sharding import PartitionSpec as P

X, Y, Z = 2, 4, 16
ZL = 4
REPS = 4
MODES = 16
KC = 256
F32 = jnp.float32
BF16 = jnp.bfloat16


def split(value):
    high = value.astype(BF16)
    return high, (value - high.astype(F32)).astype(BF16)


def tables(length):
    k = np.arange(length)[:, None]
    t = np.arange(length)[None, :]
    angle = math.pi * ((2 * k + 1) * t % (4 * length)) / (2 * length)
    forward = np.concatenate([np.cos(angle), -np.sin(angle)], axis=0).astype(np.float32)
    backward = (forward.T / length).astype(np.float32)

    def halves(table):
        high = table.astype(jnp.bfloat16)
        return high, (table - high.astype(np.float32)).astype(jnp.bfloat16)

    return np.concatenate(halves(forward), axis=1), np.concatenate(halves(backward), axis=0)


def kernel(
    proj_hbm, taps_hbm, amps_hbm, rates_hbm, skip, fwd, bwd, w_shard, out,
    proj, taps, amps, rates, ex, rev, first, ratio, wide, carry_w, rate_tiles,
    xs, halo_s, halo_r, prod, gate, local, s_send, s_recv, t_send, t_recv, starts, e_send, e_recv, p_send, p_recv,
    gall, wg, acc, o_send, o_own,
    word_sem, in_sem, halo_sem, s_ssem, s_rsem, t_ssem, t_rsem, e_ssem, e_rsem, p_ssem, p_rsem,
    wx_sem, wf_rsem, wf_ssem, wb_rsem, wbz_ssem, wz_rsem, wz_ssem, wl_rsem, wr_rsem, wy_ssem, wh_rsem, wh_ssem, g_rsem, g_ssem, f_ssem, h_ssem, o_sem,
):
    chans, length = proj.shape[1], proj.shape[2]
    groups = chans // 128
    rows = w_shard.shape[0]
    half = w_shard.shape[1] // 2
    pieces = chans // KC
    steps = length // 8

    ctx = lax.axis_index("ctx")
    rep = lax.axis_index("rep")
    z = lax.rem(ctx, Z)
    y = lax.rem(ctx // Z, Y)
    xl = ctx // (Y * Z)
    xo = 1 - xl
    rep_core = rep + 1 - 2 * lax.rem(rep, 2)
    rep_far = rep + 2 - 4 * (rep // 2)

    def at(x_, y_, z_):
        return (x_ * Y + y_) * Z + z_

    def remote(src, dst, ssem, rsem, c, r=None):
        return pltpu.make_async_remote_copy(
            src_ref=src, dst_ref=dst, send_sem=ssem, recv_sem=rsem,
            device_id=(c, rep if r is None else r), device_id_type=pl.DeviceIdType.MESH,
        )

    nxt = lax.rem(ctx + 1, X * Y * Z)
    prv = lax.rem(ctx + X * Y * Z - 1, X * Y * Z)
    zr = at(xl, y, lax.rem(z + 1, Z))
    zl = at(xl, y, lax.rem(z + Z - 1, Z))

    bar = pltpu.get_barrier_semaphore()

    def hello(c, r):
        pl.semaphore_signal(bar, inc=1, device_id=(c, r), device_id_type=pl.DeviceIdType.MESH)

    ZH = Z // ZL
    zh = z // ZL
    plane = Y * ZL
    mine = y * ZL + lax.rem(z, ZL)

    def plane_peer(q):
        return at(xl, q // ZL, zh * ZL + lax.rem(q, ZL))

    def slab_peer(x_, h):
        return at(x_, y, h * ZL + lax.rem(z, ZL))

    up = at(xl, y, lax.rem(z + ZL, Z))
    down = at(xl, y, lax.rem(z + Z - ZL, Z))
    cx = at(xo, y, z)

    @pl.loop(1, plane)
    def _(d):
        hello(plane_peer(lax.rem(mine + d, plane)), rep)

    for c in (nxt, prv, zr, zl, up, down, cx):
        hello(c, rep)
    hello(ctx, rep_core)
    hello(cx, rep_far)
    reads = [
        pltpu.make_async_copy(proj_hbm.at[i], proj.at[i], in_sem.at[i]) for i in range(3)
    ]
    reads += [
        pltpu.make_async_copy(rates_hbm, rates, in_sem.at[3]),
        pltpu.make_async_copy(amps_hbm, amps, in_sem.at[4]),
        pltpu.make_async_copy(taps_hbm, taps, in_sem.at[5]),
    ]
    for read in reads:
        read.start()

    def lanes(g, width=128):
        return pl.ds(pl.multiple_of(g * width, width), width)

    eye = (
        lax.broadcasted_iota(jnp.int32, (length, length), 0)
        == lax.broadcasted_iota(jnp.int32, (length, length), 1)
    ).astype(BF16)

    for s in range(3):
        reads[s].wait()

        @pl.loop(0, groups)
        def _(g):
            xs[s, pl.ds(8, length), lanes(g)] = lax.dot_general(
                eye, proj[s, lanes(g), :], (((1,), (1,)), ((), ())), preferred_element_type=F32
            )

        xs[s, pl.ds(0, 8), :] = jnp.zeros((8, chans), F32)
    halo_s[...] = jnp.zeros_like(halo_s)
    for s in range(3):
        halo_s[pl.ds(2 * s, 2), :] = xs[s, pl.ds(8 + length - 2, 2), :]

    pl.semaphore_wait(bar, (plane - 1) + 7 + 2)

    def pass_on(i):
        for c in (up, down):
            pl.semaphore_signal(
                word_sem.at[i], inc=1, device_id=(c, rep), device_id_type=pl.DeviceIdType.MESH
            )

    pass_on(0)
    halo = remote(halo_s, halo_r, halo_sem.at[0], halo_sem.at[1], nxt)
    halo.start()

    RZ = Z // 2
    half_rows = rows // 2
    last = half // 4 if half >= 512 else half // 2
    lead, rest = pl.ds(0, half - last), pl.ds(half - last, last)

    def wcols(i):
        return w_shard.at[:, pl.ds(pl.multiple_of(i * half, half), half)]

    x_copy = remote(wcols(xo), wg.at[xl, y, z], wx_sem.at[0], wx_sem.at[1], cx)
    x_copy.start()
    own = pltpu.make_async_copy(wcols(xl), wg.at[xl, y, z], wx_sem.at[2])
    own.start()

    def y_of(d):
        return lax.rem(y + d, Y)

    def z_of(d):
        return lax.rem(z + d + Z, Z)

    y_next, y_prev = at(xl, y_of(1), z), at(xl, y_of(Y - 1), z)

    def w_half(d_y, d_z, i, ssem, rsem, c):
        part = wg.at[:, y_of(d_y), z_of(d_z), pl.ds(i * half_rows, half_rows), lead]
        return remote(part, part, ssem, rsem.at[i * Z + z_of(d_z)], c)

    def w_round(d_z, i, right, k):
        ssem = wz_ssem.at[(i * 2 + right) * RZ + k]
        return w_half(0, d_z, i, ssem, wz_rsem, zr if right else zl)

    def w_arrived(d_z, i):
        w_half(0, d_z, i, wx_sem.at[0], wz_rsem, ctx).wait_recv()

    def w_whole(d_y, d_z, ssem, rsem, c):
        part = wg.at[:, y_of(d_y), z_of(d_z), :, lead]
        return remote(part, part, ssem, rsem.at[z_of(d_z)], c)

    def w_spread(d_z):
        w_whole(0, d_z, wy_ssem.at[z_of(d_z)], wl_rsem, y_next).start()
        w_whole(0, d_z, wy_ssem.at[Z + z_of(d_z)], wr_rsem, y_prev).start()

    def w_relay(d_z):
        w_whole(Y - 1, d_z, wx_sem.at[0], wl_rsem, ctx).wait_recv()
        w_half(Y - 1, d_z, 0, wh_ssem.at[z_of(d_z)], wh_rsem, y_next).start()
        w_whole(1, d_z, wx_sem.at[0], wr_rsem, ctx).wait_recv()
        w_half(1, d_z, 1, wh_ssem.at[Z + z_of(d_z)], wh_rsem, y_prev).start()

    def w_relayed(d_z):
        for i in range(2):
            w_half(2, d_z, i, wx_sem.at[0], wh_rsem, ctx).wait_recv()

    def b_first(d_y, ssem, c):
        part = wg.at[:, y_of(d_y), z, :, rest]
        return remote(part, part, ssem, rsem=wf_rsem.at[y_of(d_y)], c=c)

    def b_copy(p, d_z, ssem, c):
        part = wg.at[:, pl.ds(p * (Y // 2), Y // 2), z_of(d_z), :, rest]
        return remote(part, part, ssem, rsem=wb_rsem.at[p * Z + z_of(d_z)], c=c)

    def b_round(p, d_z, right, k):
        return b_copy(p, d_z, wbz_ssem.at[(p * 2 + right) * RZ + k], zr if right else zl)

    def b_arrived(p, d_z):
        b_copy(p, d_z, wx_sem.at[0], ctx).wait_recv()

    def b_step(k):
        for j in range(1, Y if k == 0 else 1):
            b_first(j, wf_ssem.at[0], ctx).wait_recv()
        for p in range(2):
            if k > 0:
                b_arrived(p, -k)
            if k < RZ - 1 or p == 0:
                b_round(p, -k, 1, k).start()
            if k > 0:
                b_arrived(p, k)
            if k < RZ - 1 or p == 1:
                b_round(p, k, 0, k).start()

    def w_start():
        own.wait()
        x_copy.wait_recv()
        for i in range(2):
            w_round(0, i, 1, 0).start()
            w_round(0, i, 0, 0).start()
        for j in range(1, Y):
            b_first(0, wf_ssem.at[j], at(xl, y_of(j), z)).start()
        w_spread(0)

    def w_step(k):
        if k >= RZ:
            return
        for i in range(2):
            w_arrived(-k, i)
            if k < RZ - 1 or i == 0:
                w_round(-k, i, 1, k).start()
            w_arrived(k, i)
            if k < RZ - 1 or i == 1:
                w_round(k, i, 0, k).start()
        w_spread(-k)
        w_spread(k)
        b_step(k - 1)
        if k > 1:
            w_relay(2 - k)
        if k > 2:
            w_relay(k - 2)

    def w_last():
        for i in range(2):
            w_arrived(RZ, i)
        w_spread(RZ)
        b_step(RZ - 1)
        for k in (RZ - 2, RZ - 1):
            w_relay(-k)
            if k > 0:
                w_relay(k)

    sub = lax.broadcasted_iota(jnp.int32, (MODES, 8, 128), 1).astype(F32)
    for read in reads[3:]:
        read.wait()

    @pl.loop(0, groups)
    def _(g):
        r2 = rates[:, lanes(g)]
        w2 = amps[:, lanes(g)] * jnp.sqrt(2.0 * r2)
        rate_tiles[g] = r2[0:8]
        rate_tiles[groups + g] = r2[8:16]
        once = w2 * jnp.exp(-r2)
        carry_w[g] = once[0:8]
        carry_w[groups + g] = once[8:16]
        r = r2[:, None, :]
        ex[:, :, lanes(g)] = jnp.exp(-r * sub)
        back = jnp.exp(-r * (7.0 - sub))
        rev[:, :, lanes(g)] = back
        first[:, :, lanes(g)] = back * jnp.exp(-float(length - 8) * r)
        ratio[:, :, lanes(g)] = jnp.exp(-8.0 * r)
        wide[:, :, lanes(g)] = w2[:, None, :]

    w_start()

    def featured(g, begin, count):
        made = []
        for s in range(3):
            total = taps[s, pl.ds(0, 1), lanes(g)] * xs[s, pl.ds(8 + begin, count), lanes(g)]
            for j in range(1, 3):
                total = total + (
                    taps[s, pl.ds(j, 1), lanes(g)]
                    * xs[s, pl.ds(8 + begin - j, count), lanes(g)]
                )
            made.append(total)
        return made[0].astype(BF16).astype(F32), (made[1] * made[2]).astype(BF16).astype(F32)

    top = lax.broadcasted_iota(jnp.int32, (8, 128), 0) < 2

    @pl.loop(0, groups)
    def _(g):
        gate_here, prod_here = featured(g, 0, length)
        gate[:, lanes(g)] = gate_here
        prod[:, lanes(g)] = prod_here
        step = ratio[:, :, lanes(g)]
        state = jnp.where(top, 0.0, prod[pl.ds(0, 8), lanes(g)])[None] * step
        for a in range(1, steps):
            state = state + prod[pl.ds(8 * a, 8), lanes(g)][None]
            if a < steps - 1:
                state = state * step
        ends = jnp.sum(state * rev[:, :, lanes(g)], axis=1)
        s_send[g] = ends[0:8]
        s_send[groups + g] = ends[8:16]

    halo.wait_recv()
    keep = jnp.where(ctx > 0, 1.0, 0.0).astype(F32)
    for s in range(3):
        xs[s, pl.ds(6, 2), :] = halo_r[pl.ds(2 * s, 2), :] * keep

    @pl.loop(0, groups)
    def _(g):
        gate_here, prod_here = featured(g, 0, 8)
        gate[pl.ds(0, 8), lanes(g)] = gate_here
        prod[pl.ds(0, 8), lanes(g)] = prod_here
        more = jnp.sum(
            first[:, :, lanes(g)] * jnp.where(top, prod_here, 0.0)[None], axis=1
        )
        s_send[g] += more[0:8]
        s_send[groups + g] += more[8:16]

    pl.semaphore_wait(word_sem.at[0], 2)
    pass_on(1)
    s_recv[mine] = s_send[mine]

    @pl.loop(1, plane)
    def _(d):
        to = lax.rem(mine + d, plane)
        remote(
            s_send.at[to], s_recv.at[mine], s_ssem.at[d], s_rsem.at[mine], plane_peer(to)
        ).start()

    w_step(1)

    @pl.loop(0, groups)
    def _(g):
        q = wide[:, :, lanes(g)] * ex[:, :, lanes(g)]
        step = ratio[:, :, lanes(g)]
        for a in range(steps):
            local[pl.ds(8 * a, 8), lanes(g)] = jnp.sum(q, axis=0)
            q = q * step

    def dot(left, right):
        return jnp.dot(left, right, preferred_element_type=F32)

    @pl.loop(0, chans // 256)
    def _(g):
        h_hi, h_lo = split(local[:, lanes(g, 256)])
        h_spec = dot(fwd[...], jnp.concatenate([h_hi, h_hi], axis=0)) + dot(fwd[:, :length], h_lo)
        u = prod[:, lanes(g, 256)]
        u_hi = u.astype(BF16)
        u_spec = dot(fwd[...], jnp.concatenate([u_hi, u_hi], axis=0))
        u_re, u_im = u_spec[:length], u_spec[length:]
        h_re, h_im = h_spec[:length], h_spec[length:]
        joint = jnp.concatenate(
            [u_re * h_re - u_im * h_im, u_re * h_im + u_im * h_re], axis=0
        )
        j_hi, j_lo = split(joint)
        mixed = dot(bwd[...], j_hi)
        mixed = mixed[:length] + mixed[length:] + dot(bwd[:length, :], j_lo)
        local[:, lanes(g, 256)] = mixed + skip[:, lanes(g, 256)] * u

    w_step(2)

    @pl.loop(1, plane)
    def _(d):
        src = lax.rem(mine + d, plane)
        remote(s_send.at[mine], s_recv.at[src], s_ssem.at[d], s_rsem.at[src], ctx).wait_recv()

    tile_rate = rate_tiles[mine]
    block_decay = jnp.exp(-float(length) * tile_rate)
    for i in range(Y):
        total = jnp.zeros((8, 128), F32)
        for j in range(ZL):
            total = total * block_decay + s_recv[i * ZL + j]
        t_send[i] = total
        t_recv[zh, i] = total
    group = float(length * ZL)
    share = jnp.zeros((8, 128), F32)
    for i in range(Y):
        left = (Y * ZH - 1 - (i * ZH + zh)).astype(F32)
        share = share + t_send[i] * jnp.exp(-(group * left) * tile_rate)
    e_send[...] = share
    pl.semaphore_wait(word_sem.at[1], 2)

    @pl.loop(1, ZH)
    def _(d):
        to = lax.rem(zh + d, ZH)
        remote(t_send, t_recv.at[zh], t_ssem.at[d], t_rsem.at[zh], slab_peer(xl, to)).start()

    @pl.loop(0, ZH)
    def _(h):
        remote(e_send, e_recv.at[zh], e_ssem.at[h], e_rsem.at[zh], slab_peer(xo, h)).start()

    w_step(3)
    w_step(4)

    @pl.loop(1, ZH)
    def _(d):
        src = lax.rem(zh + d, ZH)
        remote(t_send, t_recv.at[src], t_ssem.at[d], t_rsem.at[src], ctx).wait_recv()

    @pl.loop(0, ZH)
    def _(h):
        remote(e_send, e_recv.at[h], e_ssem.at[h], e_rsem.at[h], ctx).wait_recv()

    group_decay = jnp.exp(-group * tile_rate)
    carry = jnp.zeros((8, 128), F32)
    for j in range(Y):
        for k in range(ZH):
            starts[j * ZH + k] = carry
            carry = carry * group_decay + t_recv[k, j]
    later = jnp.zeros((8, 128), F32)
    for k in range(ZH):
        later = later + e_recv[k]
    later = jnp.where(xl > 0, later, 0.0)
    for i in range(Y):
        n = i * ZH + zh
        carry = starts[n] + later * jnp.exp(-(group * n.astype(F32)) * tile_rate)
        for j in range(ZL):
            p_send[i * ZL + j] = carry
            carry = carry * block_decay + s_recv[i * ZL + j]
    p_recv[mine] = p_send[mine]

    @pl.loop(1, plane)
    def _(d):
        to = lax.rem(mine + d, plane)
        remote(
            p_send.at[to], p_recv.at[mine], p_ssem.at[d], p_rsem.at[mine], plane_peer(to)
        ).start()

    w_step(5)
    w_step(6)

    @pl.loop(1, plane)
    def _(d):
        src = lax.rem(mine + d, plane)
        remote(p_send.at[mine], p_recv.at[src], p_ssem.at[d], p_rsem.at[src], ctx).wait_recv()

    def piece(x_, r_, k):
        return gall.at[
            r_, pl.ds(pl.multiple_of(x_ * length, length), length), pl.ds(k * KC, KC)
        ]

    def g_copy(x_, r_, k, ssem, c, r):
        return remote(
            piece(x_, r_, k), piece(x_, r_, k), ssem, g_rsem.at[(x_ * REPS + r_) * pieces + k], c, r
        )

    def g_arrived(x_, r_, k):
        g_copy(x_, r_, k, g_ssem.at[0], ctx, rep).wait_recv()

    per = KC // 128

    def finish(k):
        for i in range(per):
            g = k * per + i
            before = jnp.concatenate(
                [p_recv[g] * carry_w[g], p_recv[groups + g] * carry_w[groups + g]], axis=0
            )
            q = before[:, None, :] * ex[:, :, lanes(g)]
            step = ratio[:, :, lanes(g)]
            for a in range(steps):
                here = (pl.ds(8 * a, 8), lanes(g))
                local[here] = local[here] + jnp.sum(q, axis=0)
                q = q * step
            long = local[:, lanes(g)].astype(BF16).astype(F32)
            here = pl.ds(pl.multiple_of(xl * length, length), length)
            gall[rep, here, lanes(g)] = (gate[:, lanes(g)] * long).astype(BF16)

    for k in range(pieces):
        finish(k)
        g_copy(xl, rep, k, g_ssem.at[3 * k], ctx, rep_core).start()
        g_copy(xl, rep, k, g_ssem.at[3 * k + 1], cx, rep).start()
        g_copy(xl, rep, k, g_ssem.at[3 * k + 2], cx, rep_far).start()

    def g_pass(k):
        g_arrived(xo, rep, k)
        if k % 2 == 0:
            g_copy(xo, rep, k, h_ssem.at[k], cx, rep_far).start()
        g_copy(xo, rep, k, f_ssem.at[3 * k], ctx, rep_core).start()
        g_arrived(xo, rep_far, k)
        if k % 2 == 1:
            g_copy(xo, rep_far, k, h_ssem.at[k], cx, rep).start()
        g_copy(xo, rep_far, k, f_ssem.at[3 * k + 1], ctx, rep_core).start()

    w_step(7)
    for k in range(pieces // 2):
        g_pass(k)
    w_last()
    for k in range(pieces // 2, pieces):
        g_pass(k)
    for p in range(2):
        b_arrived(p, RZ)
    w_relay(RZ)

    @pl.loop(0, Z)
    def _(d):
        w_relayed(d)

    def project(r_, here):
        n = r_ * (chans // rows) // Z
        part = wg[n // Y, pl.ds(lax.rem(n, Y), chans // rows // Z)].reshape(chans, half)
        return jnp.dot(gall[r_, here, :], part, preferred_element_type=F32)

    both = pl.ds(0, X * length)
    acc[...] = project(rep, both)

    @pl.loop(0, pieces)
    def _(k):
        g_arrived(xl, rep_far, k)
        g_copy(xl, rep_far, k, f_ssem.at[3 * k + 2], ctx, rep_core).start()

    acc[...] += project(rep_far, both)
    core_far = rep_far + rep_core - rep

    @pl.loop(0, pieces)
    def _(k):
        for x_ in range(X):
            g_arrived(x_, rep_core, k)

    acc[...] += project(rep_core, both)

    @pl.loop(0, pieces)
    def _(k):
        for x_ in range(X):
            g_arrived(x_, core_far, k)

    def turn(x_, to):
        here = pl.ds(pl.multiple_of(x_ * length, length), length)
        acc[here, :] += project(core_far, here)
        for i in range(half // 128):
            cols = pl.ds(128 * i, 128)
            to[cols, :] = acc[here, cols].T.astype(BF16)

    turn(xo, o_send)
    swap = remote(o_send, out.at[xl], o_sem.at[0], o_sem.at[1], cx)
    swap.start()
    turn(xl, o_own)
    keep_own = pltpu.make_async_copy(o_own, out.at[xl], o_sem.at[2])
    keep_own.start()

    halo.wait_send()
    x_copy.wait_send()

    @pl.loop(1, plane)
    def _(d):
        remote(s_send.at[0], s_recv.at[0], s_ssem.at[d], s_rsem.at[0], ctx).wait_send()
        remote(p_send.at[0], p_recv.at[0], p_ssem.at[d], p_rsem.at[0], ctx).wait_send()

    @pl.loop(1, ZH)
    def _(d):
        remote(t_send, t_recv.at[0], t_ssem.at[d], t_rsem.at[0], ctx).wait_send()

    @pl.loop(0, ZH)
    def _(h):
        remote(e_send, e_recv.at[0], e_ssem.at[h], e_rsem.at[0], ctx).wait_send()

    @pl.loop(0, Z)
    def _(i):
        for j in range(2):
            w_whole(0, 0, wy_ssem.at[j * Z + i], wl_rsem, ctx).wait_send()
            w_half(0, 0, 0, wh_ssem.at[j * Z + i], wh_rsem, ctx).wait_send()

    for j in range(1, Y):
        b_first(0, wf_ssem.at[j], ctx).wait_send()
    for k in range(RZ):
        for i in range(2):
            for right in range(2):
                if k < RZ - 1 or i != right:
                    w_round(0, i, right, k).wait_send()
                    b_round(i, 0, right, k).wait_send()

    @pl.loop(0, 3 * pieces)
    def _(i):
        g_copy(0, 0, 0, g_ssem.at[i], ctx, rep).wait_send()
        g_copy(0, 0, 0, f_ssem.at[i], ctx, rep).wait_send()

    @pl.loop(0, pieces)
    def _(i):
        g_copy(0, 0, 0, h_ssem.at[i], ctx, rep).wait_send()

    keep_own.wait()
    swap.wait_send()
    remote(o_send, out.at[xo], o_sem.at[0], o_sem.at[1], ctx).wait_recv()


def per_device(projected, short_taps, residues, decay_rates, skip_gain, out_weight):
    _, chans, length = projected.shape
    groups = chans // 128
    rows, feats = out_weight.shape
    half = feats // X
    pieces = chans // KC
    fwd, bwd = tables(length)
    vm = pltpu.VMEM
    dma = pltpu.SemaphoreType.DMA
    out = pl.pallas_call(
        kernel,
        out_shape=jax.ShapeDtypeStruct((X, half, length), BF16),
        in_specs=[pl.BlockSpec(memory_space=pltpu.HBM)] * 4
        + [pl.BlockSpec(memory_space=vm)] * 3
        + [pl.BlockSpec(memory_space=pltpu.HBM)],
        out_specs=pl.BlockSpec(memory_space=pl.ANY),
        scratch_shapes=[
            vm((3, chans, length), BF16),
            vm((3, 3, chans), F32),
            vm((MODES, chans), F32),
            vm((MODES, chans), F32),
            vm((MODES, 8, chans), F32),
            vm((MODES, 8, chans), F32),
            vm((MODES, 8, chans), F32),
            vm((MODES, 1, chans), F32),
            vm((MODES, 1, chans), F32),
            vm((Y * ZL, 8, 128), F32),
            vm((Y * ZL, 8, 128), F32),
            vm((3, length + 8, chans), F32),
            vm((8, chans), F32),
            vm((8, chans), F32),
            vm((length, chans), F32),
            vm((length, chans), F32),
            vm((length, chans), F32),
            vm((Y * ZL, 8, 128), F32),
            vm((Y * ZL, 8, 128), F32),
            vm((Y, 8, 128), F32),
            vm((Z // ZL, Y, 8, 128), F32),
            vm((Y * Z // ZL, 8, 128), F32),
            vm((8, 128), F32),
            vm((Z // ZL, 8, 128), F32),
            vm((Y * ZL, 8, 128), F32),
            vm((Y * ZL, 8, 128), F32),
            vm((REPS, X * length, chans), BF16),
            vm((X, Y, Z, rows, half), BF16),
            vm((X * length, half), F32),
            vm((half, length), BF16),
            vm((half, length), BF16),
            pltpu.SemaphoreType.REGULAR((2,)),
            dma((6,)),
            dma((2,)),
            dma((Y * ZL,)),
            dma((Y * ZL,)),
            dma((Z // ZL,)),
            dma((Z // ZL,)),
            dma((Z // ZL,)),
            dma((Z // ZL,)),
            dma((Y * ZL,)),
            dma((Y * ZL,)),
            dma((3,)),
            dma((Y,)),
            dma((Y,)),
            dma((2 * Z,)),
            dma((2 * Z,)),
            dma((2 * Z,)),
            dma((2 * Z,)),
            dma((Z,)),
            dma((Z,)),
            dma((2 * Z,)),
            dma((2 * Z,)),
            dma((2 * Z,)),
            dma((X * REPS * pieces,)),
            dma((3 * pieces,)),
            dma((3 * pieces,)),
            dma((pieces,)),
            dma((3,)),
        ],
        compiler_params=pltpu.CompilerParams(
            collective_id=0, has_side_effects=True, vmem_limit_bytes=60 * 1024 * 1024
        ),
        name="hyena",
    )(
        projected, short_taps.transpose(0, 2, 1), residues.T, decay_rates.T, skip_gain[None],
        jnp.asarray(fwd), jnp.asarray(bwd), out_weight,
    )
    return out.reshape(feats, length)


def solution(mesh):
    in_specs = (
        P(None, "rep", "ctx"),
        P(None, "rep", None),
        P("rep", None),
        P("rep", None),
        P("rep"),
        P("ctx", "rep"),
    )
    out_specs = P("rep", "ctx")
    return jax.shard_map(
        per_device, mesh=mesh, in_specs=in_specs, out_specs=out_specs, check_vma=False
    )
```

```python
import math

import numpy as np
import jax
import jax.numpy as jnp
from jax import lax
from jax.experimental import pallas as pl
from jax.experimental.pallas import tpu as pltpu
from jax.sharding import PartitionSpec as P

X, Y, Z = 2, 4, 16
ZL = 4
REPS = 4
MODES = 16
KC = 256
F32 = jnp.float32
BF16 = jnp.bfloat16


def split(value):
    high = value.astype(BF16)
    return high, (value - high.astype(F32)).astype(BF16)


def tables(length):
    k = np.arange(length)[:, None]
    t = np.arange(length)[None, :]
    angle = math.pi * ((2 * k + 1) * t % (4 * length)) / (2 * length)
    forward = np.concatenate([np.cos(angle), -np.sin(angle)], axis=0).astype(np.float32)
    backward = (forward.T / length).astype(np.float32)

    def halves(table):
        high = table.astype(jnp.bfloat16)
        return high, (table - high.astype(np.float32)).astype(jnp.bfloat16)

    return np.concatenate(halves(forward), axis=1), np.concatenate(halves(backward), axis=0)


def kernel(
    proj_hbm, taps_hbm, amps_hbm, rates_hbm, skip, fwd, bwd, w_shard, out,
    proj, taps, amps, rates, ex, rev, first, ratio, wide, carry_w, rate_tiles,
    xs, halo_s, halo_r, prod, gate, local, s_send, s_recv, t_send, t_recv, starts, e_send, e_recv, p_send, p_recv,
    gall, wg, acc, o_send,
    word_sem, in_sem, halo_sem, s_ssem, s_rsem, t_ssem, t_rsem, e_ssem, e_rsem, p_ssem, p_rsem,
    wx_sem, wf_rsem, wf_ssem, wb_rsem, wbz_ssem, wz_rsem, wz_ssem, wl_rsem, wr_rsem, wy_ssem, wh_rsem, wh_ssem, g_rsem, g_ssem, f_ssem, h_ssem, o_sem,
):
    chans, length = proj.shape[1], proj.shape[2]
    groups = chans // 128
    rows = w_shard.shape[0]
    half = w_shard.shape[1] // 2
    pieces = chans // KC
    steps = length // 8

    ctx = lax.axis_index("ctx")
    rep = lax.axis_index("rep")
    z = lax.rem(ctx, Z)
    y = lax.rem(ctx // Z, Y)
    xl = ctx // (Y * Z)
    xo = 1 - xl
    rep_core = rep + 1 - 2 * lax.rem(rep, 2)
    rep_far = rep + 2 - 4 * (rep // 2)

    def at(x_, y_, z_):
        return (x_ * Y + y_) * Z + z_

    def remote(src, dst, ssem, rsem, c, r=None):
        return pltpu.make_async_remote_copy(
            src_ref=src, dst_ref=dst, send_sem=ssem, recv_sem=rsem,
            device_id=(c, rep if r is None else r), device_id_type=pl.DeviceIdType.MESH,
        )

    nxt = lax.rem(ctx + 1, X * Y * Z)
    prv = lax.rem(ctx + X * Y * Z - 1, X * Y * Z)
    zr = at(xl, y, lax.rem(z + 1, Z))
    zl = at(xl, y, lax.rem(z + Z - 1, Z))

    bar = pltpu.get_barrier_semaphore()

    def hello(c, r):
        pl.semaphore_signal(bar, inc=1, device_id=(c, r), device_id_type=pl.DeviceIdType.MESH)

    ZH = Z // ZL
    zh = z // ZL
    plane = Y * ZL
    mine = y * ZL + lax.rem(z, ZL)

    def plane_peer(q):
        return at(xl, q // ZL, zh * ZL + lax.rem(q, ZL))

    def slab_peer(x_, h):
        return at(x_, y, h * ZL + lax.rem(z, ZL))

    up = at(xl, y, lax.rem(z + ZL, Z))
    down = at(xl, y, lax.rem(z + Z - ZL, Z))
    cx = at(xo, y, z)

    for c in (up, down, nxt, prv, zr, zl):
        hello(c, rep)

    @pl.loop(1, plane)
    def _(d):
        hello(plane_peer(lax.rem(mine + d, plane)), rep)

    hello(cx, rep)
    hello(ctx, rep_core)
    hello(cx, rep_far)
    reads = [
        pltpu.make_async_copy(proj_hbm.at[i], proj.at[i], in_sem.at[i]) for i in range(3)
    ]
    reads += [
        pltpu.make_async_copy(rates_hbm, rates, in_sem.at[3]),
        pltpu.make_async_copy(amps_hbm, amps, in_sem.at[4]),
        pltpu.make_async_copy(taps_hbm, taps, in_sem.at[5]),
    ]
    for read in reads:
        read.start()

    def lanes(g, width=128):
        return pl.ds(pl.multiple_of(g * width, width), width)

    eye = (
        lax.broadcasted_iota(jnp.int32, (length, length), 0)
        == lax.broadcasted_iota(jnp.int32, (length, length), 1)
    ).astype(BF16)

    for s in range(3):
        reads[s].wait()

        @pl.loop(0, groups)
        def _(g):
            xs[s, pl.ds(8, length), lanes(g)] = lax.dot_general(
                eye, proj[s, lanes(g), :], (((1,), (1,)), ((), ())), preferred_element_type=F32
            )

        xs[s, pl.ds(0, 8), :] = jnp.zeros((8, chans), F32)
    halo_s[...] = jnp.zeros_like(halo_s)
    for s in range(3):
        halo_s[pl.ds(2 * s, 2), :] = xs[s, pl.ds(8 + length - 2, 2), :]

    pl.semaphore_wait(bar, (plane - 1) + 7 + 2)

    def pass_on(i):
        for c in (up, down):
            pl.semaphore_signal(
                word_sem.at[i], inc=1, device_id=(c, rep), device_id_type=pl.DeviceIdType.MESH
            )

    pass_on(0)
    halo = remote(halo_s, halo_r, halo_sem.at[0], halo_sem.at[1], nxt)
    halo.start()

    RZ = Z // 2
    half_rows = rows // 2
    last = half // 4 if half >= 512 else half // 2
    lead, rest = pl.ds(0, half - last), pl.ds(half - last, last)

    def wcols(i):
        return w_shard.at[:, pl.ds(pl.multiple_of(i * half, half), half)]

    x_copy = remote(wcols(xo), wg.at[xl, y, z], wx_sem.at[0], wx_sem.at[1], cx)
    x_copy.start()
    own = pltpu.make_async_copy(wcols(xl), wg.at[xl, y, z], wx_sem.at[2])
    own.start()

    def y_of(d):
        return lax.rem(y + d, Y)

    def z_of(d):
        return lax.rem(z + d + Z, Z)

    y_next, y_prev = at(xl, y_of(1), z), at(xl, y_of(Y - 1), z)

    def w_half(d_y, d_z, i, ssem, rsem, c):
        part = wg.at[:, y_of(d_y), z_of(d_z), pl.ds(i * half_rows, half_rows), lead]
        return remote(part, part, ssem, rsem.at[i * Z + z_of(d_z)], c)

    def w_round(d_z, i, right, k):
        ssem = wz_ssem.at[(i * 2 + right) * RZ + k]
        return w_half(0, d_z, i, ssem, wz_rsem, zr if right else zl)

    def w_arrived(d_z, i):
        w_half(0, d_z, i, wx_sem.at[0], wz_rsem, ctx).wait_recv()

    def w_whole(d_y, d_z, ssem, rsem, c):
        part = wg.at[:, y_of(d_y), z_of(d_z), :, lead]
        return remote(part, part, ssem, rsem.at[z_of(d_z)], c)

    def w_spread(d_z):
        w_whole(0, d_z, wy_ssem.at[z_of(d_z)], wl_rsem, y_next).start()
        w_whole(0, d_z, wy_ssem.at[Z + z_of(d_z)], wr_rsem, y_prev).start()

    def w_relay(d_z):
        w_whole(Y - 1, d_z, wx_sem.at[0], wl_rsem, ctx).wait_recv()
        w_half(Y - 1, d_z, 0, wh_ssem.at[z_of(d_z)], wh_rsem, y_next).start()
        w_whole(1, d_z, wx_sem.at[0], wr_rsem, ctx).wait_recv()
        w_half(1, d_z, 1, wh_ssem.at[Z + z_of(d_z)], wh_rsem, y_prev).start()

    def w_relayed(d_z):
        for i in range(2):
            w_half(2, d_z, i, wx_sem.at[0], wh_rsem, ctx).wait_recv()

    def b_first(d_y, ssem, c):
        part = wg.at[:, y_of(d_y), z, :, rest]
        return remote(part, part, ssem, rsem=wf_rsem.at[y_of(d_y)], c=c)

    def b_copy(p, d_z, ssem, c):
        part = wg.at[:, pl.ds(p * (Y // 2), Y // 2), z_of(d_z), :, rest]
        return remote(part, part, ssem, rsem=wb_rsem.at[p * Z + z_of(d_z)], c=c)

    def b_round(p, d_z, right, k):
        return b_copy(p, d_z, wbz_ssem.at[(p * 2 + right) * RZ + k], zr if right else zl)

    def b_arrived(p, d_z):
        b_copy(p, d_z, wx_sem.at[0], ctx).wait_recv()

    def b_step(k):
        for j in range(1, Y if k == 0 else 1):
            b_first(j, wf_ssem.at[0], ctx).wait_recv()
        for p in range(2):
            if k > 0:
                b_arrived(p, -k)
            if k < RZ - 1 or p == 0:
                b_round(p, -k, 1, k).start()
            if k > 0:
                b_arrived(p, k)
            if k < RZ - 1 or p == 1:
                b_round(p, k, 0, k).start()

    def w_direct(d_z):
        for i in range(2):
            ssem = wh_ssem.at[i * Z + z_of(d_z)]
            w_half(0, d_z, i, ssem, wh_rsem, at(xl, y_of(2), z)).start()

    def w_sides(d_z):
        w_whole(Y - 1, d_z, wx_sem.at[0], wl_rsem, ctx).wait_recv()
        w_whole(1, d_z, wx_sem.at[0], wr_rsem, ctx).wait_recv()

    def w_start():
        own.wait()
        x_copy.wait_recv()
        for i in range(2):
            w_round(0, i, 1, 0).start()
            w_round(0, i, 0, 0).start()
        for j in range(1, Y):
            b_first(0, wf_ssem.at[j], at(xl, y_of(j), z)).start()
        w_spread(0)

    def w_step(k):
        if k >= RZ:
            return
        for i in range(2):
            w_arrived(-k, i)
            if k < RZ - 1 or i == 0:
                w_round(-k, i, 1, k).start()
            w_arrived(k, i)
            if k < RZ - 1 or i == 1:
                w_round(k, i, 0, k).start()
        b_step(k - 1)
        w_spread(-k)
        w_spread(k)
        if k > 1:
            w_relay(2 - k)
        if k > 2:
            w_relay(k - 2)

    def w_last():
        for i in range(2):
            w_arrived(RZ, i)
        w_direct(RZ)
        w_spread(RZ)
        b_step(RZ - 1)
        for k in (RZ - 2, RZ - 1):
            w_relay(-k)
            if k > 0:
                w_relay(k)

    sub = lax.broadcasted_iota(jnp.int32, (MODES, 8, 128), 1).astype(F32)
    for read in reads[3:]:
        read.wait()

    @pl.loop(0, groups)
    def _(g):
        r2 = rates[:, lanes(g)]
        w2 = amps[:, lanes(g)] * jnp.sqrt(2.0 * r2)
        rate_tiles[g] = r2[0:8]
        rate_tiles[groups + g] = r2[8:16]
        once = w2 * jnp.exp(-r2)
        carry_w[g] = once[0:8]
        carry_w[groups + g] = once[8:16]
        r = r2[:, None, :]
        ex[:, :, lanes(g)] = jnp.exp(-r * sub)
        back = jnp.exp(-r * (7.0 - sub))
        rev[:, :, lanes(g)] = back
        first[:, :, lanes(g)] = back * jnp.exp(-float(length - 8) * r)
        ratio[:, :, lanes(g)] = jnp.exp(-8.0 * r)
        wide[:, :, lanes(g)] = w2[:, None, :]

    w_start()

    def featured(g, begin, count):
        made = []
        for s in range(3):
            total = taps[s, pl.ds(0, 1), lanes(g)] * xs[s, pl.ds(8 + begin, count), lanes(g)]
            for j in range(1, 3):
                total = total + (
                    taps[s, pl.ds(j, 1), lanes(g)]
                    * xs[s, pl.ds(8 + begin - j, count), lanes(g)]
                )
            made.append(total)
        return made[0].astype(BF16).astype(F32), (made[1] * made[2]).astype(BF16).astype(F32)

    top = lax.broadcasted_iota(jnp.int32, (8, 128), 0) < 2

    @pl.loop(0, groups)
    def _(g):
        gate_here, prod_here = featured(g, 0, length)
        gate[:, lanes(g)] = gate_here
        prod[:, lanes(g)] = prod_here
        step = ratio[:, :, lanes(g)]
        state = jnp.where(top, 0.0, prod[pl.ds(0, 8), lanes(g)])[None] * step
        for a in range(1, steps):
            state = state + prod[pl.ds(8 * a, 8), lanes(g)][None]
            if a < steps - 1:
                state = state * step
        ends = jnp.sum(state * rev[:, :, lanes(g)], axis=1)
        s_send[g] = ends[0:8]
        s_send[groups + g] = ends[8:16]

    halo.wait_recv()
    keep = jnp.where(ctx > 0, 1.0, 0.0).astype(F32)
    for s in range(3):
        xs[s, pl.ds(6, 2), :] = halo_r[pl.ds(2 * s, 2), :] * keep

    @pl.loop(0, groups)
    def _(g):
        gate_here, prod_here = featured(g, 0, 8)
        gate[pl.ds(0, 8), lanes(g)] = gate_here
        prod[pl.ds(0, 8), lanes(g)] = prod_here
        more = jnp.sum(
            first[:, :, lanes(g)] * jnp.where(top, prod_here, 0.0)[None], axis=1
        )
        s_send[g] += more[0:8]
        s_send[groups + g] += more[8:16]

    pl.semaphore_wait(word_sem.at[0], 2)
    pass_on(1)
    s_recv[mine] = s_send[mine]

    @pl.loop(1, plane)
    def _(d):
        to = lax.rem(mine + d, plane)
        remote(
            s_send.at[to], s_recv.at[mine], s_ssem.at[d], s_rsem.at[mine], plane_peer(to)
        ).start()

    w_step(1)

    @pl.loop(0, groups)
    def _(g):
        q = wide[:, :, lanes(g)] * ex[:, :, lanes(g)]
        step = ratio[:, :, lanes(g)]
        for a in range(steps):
            local[pl.ds(8 * a, 8), lanes(g)] = jnp.sum(q, axis=0)
            q = q * step

    def dot(left, right):
        return jnp.dot(left, right, preferred_element_type=F32)

    @pl.loop(0, chans // 256)
    def _(g):
        h_hi, h_lo = split(local[:, lanes(g, 256)])
        h_spec = dot(fwd[...], jnp.concatenate([h_hi, h_hi], axis=0)) + dot(fwd[:, :length], h_lo)
        u = prod[:, lanes(g, 256)]
        u_hi = u.astype(BF16)
        u_spec = dot(fwd[...], jnp.concatenate([u_hi, u_hi], axis=0))
        u_re, u_im = u_spec[:length], u_spec[length:]
        h_re, h_im = h_spec[:length], h_spec[length:]
        joint = jnp.concatenate(
            [u_re * h_re - u_im * h_im, u_re * h_im + u_im * h_re], axis=0
        )
        j_hi, j_lo = split(joint)
        mixed = dot(bwd[...], j_hi)
        mixed = mixed[:length] + mixed[length:] + dot(bwd[:length, :], j_lo)
        local[:, lanes(g, 256)] = mixed + skip[:, lanes(g, 256)] * u

    w_step(2)

    @pl.loop(1, plane)
    def _(d):
        src = lax.rem(mine + d, plane)
        remote(s_send.at[mine], s_recv.at[src], s_ssem.at[d], s_rsem.at[src], ctx).wait_recv()

    tile_rate = rate_tiles[mine]
    block_decay = jnp.exp(-float(length) * tile_rate)
    for i in range(Y):
        total = jnp.zeros((8, 128), F32)
        for j in range(ZL):
            total = total * block_decay + s_recv[i * ZL + j]
        t_send[i] = total
        t_recv[zh, i] = total
    group = float(length * ZL)
    share = jnp.zeros((8, 128), F32)
    for i in range(Y):
        left = (Y * ZH - 1 - (i * ZH + zh)).astype(F32)
        share = share + t_send[i] * jnp.exp(-(group * left) * tile_rate)
    e_send[...] = share
    pl.semaphore_wait(word_sem.at[1], 2)

    for d in (2, 1, 3):
        to = lax.rem(zh + d, ZH)
        remote(t_send, t_recv.at[zh], t_ssem.at[d], t_rsem.at[zh], slab_peer(xl, to)).start()

    @pl.loop(0, ZH)
    def _(h):
        remote(e_send, e_recv.at[zh], e_ssem.at[h], e_rsem.at[zh], slab_peer(xo, h)).start()

    w_step(3)
    w_step(4)

    @pl.loop(1, ZH)
    def _(d):
        src = lax.rem(zh + d, ZH)
        remote(t_send, t_recv.at[src], t_ssem.at[d], t_rsem.at[src], ctx).wait_recv()

    @pl.loop(0, ZH)
    def _(h):
        remote(e_send, e_recv.at[h], e_ssem.at[h], e_rsem.at[h], ctx).wait_recv()

    group_decay = jnp.exp(-group * tile_rate)
    carry = jnp.zeros((8, 128), F32)
    for j in range(Y):
        for k in range(ZH):
            starts[j * ZH + k] = carry
            carry = carry * group_decay + t_recv[k, j]
    later = jnp.zeros((8, 128), F32)
    for k in range(ZH):
        later = later + e_recv[k]
    later = jnp.where(xl > 0, later, 0.0)
    for i in range(Y):
        n = i * ZH + zh
        carry = starts[n] + later * jnp.exp(-(group * n.astype(F32)) * tile_rate)
        for j in range(ZL):
            p_send[i * ZL + j] = carry
            carry = carry * block_decay + s_recv[i * ZL + j]
    p_recv[mine] = p_send[mine]

    @pl.loop(1, plane)
    def _(d):
        to = lax.rem(mine + d, plane)
        remote(
            p_send.at[to], p_recv.at[mine], p_ssem.at[d], p_rsem.at[mine], plane_peer(to)
        ).start()

    w_step(5)
    w_step(6)

    @pl.loop(1, plane)
    def _(d):
        src = lax.rem(mine + d, plane)
        remote(p_send.at[mine], p_recv.at[src], p_ssem.at[d], p_rsem.at[src], ctx).wait_recv()

    def piece(x_, r_, k):
        return gall.at[
            r_, pl.ds(pl.multiple_of(x_ * length, length), length), pl.ds(k * KC, KC)
        ]

    def g_copy(x_, r_, k, ssem, c, r):
        return remote(
            piece(x_, r_, k), piece(x_, r_, k), ssem, g_rsem.at[(x_ * REPS + r_) * pieces + k], c, r
        )

    def g_arrived(x_, r_, k):
        g_copy(x_, r_, k, g_ssem.at[0], ctx, rep).wait_recv()

    per = KC // 128

    def finish(k):
        for i in range(per):
            g = k * per + i
            before = jnp.concatenate(
                [p_recv[g] * carry_w[g], p_recv[groups + g] * carry_w[groups + g]], axis=0
            )
            q = before[:, None, :] * ex[:, :, lanes(g)]
            step = ratio[:, :, lanes(g)]
            for a in range(steps):
                here = (pl.ds(8 * a, 8), lanes(g))
                local[here] = local[here] + jnp.sum(q, axis=0)
                q = q * step
            long = local[:, lanes(g)].astype(BF16).astype(F32)
            here = pl.ds(pl.multiple_of(xl * length, length), length)
            gall[rep, here, lanes(g)] = (gate[:, lanes(g)] * long).astype(BF16)

    for k in range(pieces):
        finish(k)
        g_copy(xl, rep, k, g_ssem.at[3 * k], ctx, rep_core).start()
        g_copy(xl, rep, k, g_ssem.at[3 * k + 1], cx, rep).start()
        g_copy(xl, rep, k, g_ssem.at[3 * k + 2], cx, rep_far).start()

    def g_pass(k):
        g_arrived(xo, rep, k)
        if k % 2 == 0:
            g_copy(xo, rep, k, h_ssem.at[k], cx, rep_far).start()
        g_copy(xo, rep, k, f_ssem.at[3 * k], ctx, rep_core).start()
        g_arrived(xo, rep_far, k)
        if k % 2 == 1:
            g_copy(xo, rep_far, k, h_ssem.at[k], cx, rep).start()
        g_copy(xo, rep_far, k, f_ssem.at[3 * k + 1], ctx, rep_core).start()

    w_step(7)
    for k in range(pieces // 2):
        g_pass(k)
    w_last()
    for k in range(pieces // 2, pieces):
        g_pass(k)
    for p in range(2):
        b_arrived(p, RZ)
    w_sides(RZ)

    @pl.loop(0, Z)
    def _(d):
        w_relayed(d)

    def project(r_, here):
        n = r_ * (chans // rows) // Z
        part = wg[n // Y, pl.ds(lax.rem(n, Y), chans // rows // Z)].reshape(chans, half)
        return jnp.dot(gall[r_, here, :], part, preferred_element_type=F32)

    both = pl.ds(0, X * length)
    acc[...] = project(rep, both)

    @pl.loop(0, pieces)
    def _(k):
        g_arrived(xl, rep_far, k)
        g_copy(xl, rep_far, k, f_ssem.at[3 * k + 2], ctx, rep_core).start()

    acc[...] += project(rep_far, both)
    core_far = rep_far + rep_core - rep

    @pl.loop(0, pieces)
    def _(k):
        for x_ in range(X):
            g_arrived(x_, rep_core, k)

    acc[...] += project(rep_core, both)

    @pl.loop(0, pieces)
    def _(k):
        for x_ in range(X):
            g_arrived(x_, core_far, k)

    def turn(x_, to):
        here = pl.ds(pl.multiple_of(x_ * length, length), length)
        acc[here, :] += project(core_far, here)
        for i in range(half // 128):
            cols = pl.ds(128 * i, 128)
            to[cols, :] = acc[here, cols].T.astype(BF16)

    turn(xo, o_send)
    swap = remote(o_send, out.at[xl], o_sem.at[0], o_sem.at[1], cx)
    swap.start()
    turn(xl, out.at[xl])

    halo.wait_send()
    x_copy.wait_send()

    @pl.loop(1, plane)
    def _(d):
        remote(s_send.at[0], s_recv.at[0], s_ssem.at[d], s_rsem.at[0], ctx).wait_send()
        remote(p_send.at[0], p_recv.at[0], p_ssem.at[d], p_rsem.at[0], ctx).wait_send()

    @pl.loop(1, ZH)
    def _(d):
        remote(t_send, t_recv.at[0], t_ssem.at[d], t_rsem.at[0], ctx).wait_send()

    @pl.loop(0, ZH)
    def _(h):
        remote(e_send, e_recv.at[0], e_ssem.at[h], e_rsem.at[0], ctx).wait_send()

    @pl.loop(0, Z)
    def _(i):
        for j in range(2):
            w_whole(0, 0, wy_ssem.at[j * Z + i], wl_rsem, ctx).wait_send()
            w_half(0, 0, 0, wh_ssem.at[j * Z + i], wh_rsem, ctx).wait_send()

    for j in range(1, Y):
        b_first(0, wf_ssem.at[j], ctx).wait_send()
    for k in range(RZ):
        for i in range(2):
            for right in range(2):
                if k < RZ - 1 or i != right:
                    w_round(0, i, right, k).wait_send()
                    b_round(i, 0, right, k).wait_send()

    @pl.loop(0, 3 * pieces)
    def _(i):
        g_copy(0, 0, 0, g_ssem.at[i], ctx, rep).wait_send()
        g_copy(0, 0, 0, f_ssem.at[i], ctx, rep).wait_send()

    @pl.loop(0, pieces)
    def _(i):
        g_copy(0, 0, 0, h_ssem.at[i], ctx, rep).wait_send()

    swap.wait_send()
    remote(o_send, out.at[xo], o_sem.at[0], o_sem.at[1], ctx).wait_recv()


def per_device(projected, short_taps, residues, decay_rates, skip_gain, out_weight):
    _, chans, length = projected.shape
    groups = chans // 128
    rows, feats = out_weight.shape
    half = feats // X
    pieces = chans // KC
    fwd, bwd = tables(length)
    vm = pltpu.VMEM
    dma = pltpu.SemaphoreType.DMA
    out = pl.pallas_call(
        kernel,
        out_shape=pltpu.VMEM((X, half, length), BF16),
        in_specs=[pl.BlockSpec(memory_space=pltpu.HBM)] * 4
        + [pl.BlockSpec(memory_space=vm)] * 3
        + [pl.BlockSpec(memory_space=pltpu.HBM)],
        out_specs=pl.BlockSpec(memory_space=vm),
        scratch_shapes=[
            vm((3, chans, length), BF16),
            vm((3, 3, chans), F32),
            vm((MODES, chans), F32),
            vm((MODES, chans), F32),
            vm((MODES, 8, chans), F32),
            vm((MODES, 8, chans), F32),
            vm((MODES, 8, chans), F32),
            vm((MODES, 1, chans), F32),
            vm((MODES, 1, chans), F32),
            vm((Y * ZL, 8, 128), F32),
            vm((Y * ZL, 8, 128), F32),
            vm((3, length + 8, chans), F32),
            vm((8, chans), F32),
            vm((8, chans), F32),
            vm((length, chans), F32),
            vm((length, chans), F32),
            vm((length, chans), F32),
            vm((Y * ZL, 8, 128), F32),
            vm((Y * ZL, 8, 128), F32),
            vm((Y, 8, 128), F32),
            vm((Z // ZL, Y, 8, 128), F32),
            vm((Y * Z // ZL, 8, 128), F32),
            vm((8, 128), F32),
            vm((Z // ZL, 8, 128), F32),
            vm((Y * ZL, 8, 128), F32),
            vm((Y * ZL, 8, 128), F32),
            vm((REPS, X * length, chans), BF16),
            vm((X, Y, Z, rows, half), BF16),
            vm((X * length, half), F32),
            vm((half, length), BF16),
            pltpu.SemaphoreType.REGULAR((2,)),
            dma((6,)),
            dma((2,)),
            dma((Y * ZL,)),
            dma((Y * ZL,)),
            dma((Z // ZL,)),
            dma((Z // ZL,)),
            dma((Z // ZL,)),
            dma((Z // ZL,)),
            dma((Y * ZL,)),
            dma((Y * ZL,)),
            dma((3,)),
            dma((Y,)),
            dma((Y,)),
            dma((2 * Z,)),
            dma((2 * Z,)),
            dma((2 * Z,)),
            dma((2 * Z,)),
            dma((Z,)),
            dma((Z,)),
            dma((2 * Z,)),
            dma((2 * Z,)),
            dma((2 * Z,)),
            dma((X * REPS * pieces,)),
            dma((3 * pieces,)),
            dma((3 * pieces,)),
            dma((pieces,)),
            dma((2,)),
        ],
        compiler_params=pltpu.CompilerParams(
            collective_id=0, has_side_effects=True, vmem_limit_bytes=60 * 1024 * 1024
        ),
        name="hyena",
    )(
        projected, short_taps.transpose(0, 2, 1), residues.T, decay_rates.T, skip_gain[None],
        jnp.asarray(fwd), jnp.asarray(bwd), out_weight,
    )
    return out.reshape(feats, length)


def solution(mesh):
    in_specs = (
        P(None, "rep", "ctx"),
        P(None, "rep", None),
        P("rep", None),
        P("rep", None),
        P("rep"),
        P("ctx", "rep"),
    )
    out_specs = P("rep", "ctx")
    return jax.shard_map(
        per_device, mesh=mesh, in_specs=in_specs, out_specs=out_specs, check_vma=False
    )
```

```python
import math

import numpy as np
import jax
import jax.numpy as jnp
from jax import lax
from jax.experimental import pallas as pl
from jax.experimental.pallas import tpu as pltpu
from jax.sharding import PartitionSpec as P

X, Y, Z = 2, 4, 16
ZL = 4
REPS = 4
MODES = 16
KC = 512
F32 = jnp.float32
BF16 = jnp.bfloat16


def split(value):
    high = value.astype(BF16)
    return high, (value - high.astype(F32)).astype(BF16)


def tables(length):
    k = np.arange(length)[:, None]
    t = np.arange(length)[None, :]
    angle = math.pi * ((2 * k + 1) * t % (4 * length)) / (2 * length)
    forward = np.concatenate([np.cos(angle), -np.sin(angle)], axis=0).astype(np.float32)
    backward = (forward.T / length).astype(np.float32)

    def halves(table):
        high = table.astype(jnp.bfloat16)
        return high, (table - high.astype(np.float32)).astype(jnp.bfloat16)

    return np.concatenate(halves(forward), axis=1), np.concatenate(halves(backward), axis=0)


def kernel(
    proj_hbm, taps_hbm, amps_hbm, rates_hbm, skip, fwd, bwd, w_shard, out,
    proj, taps, amps, rates, ex, rev, first, ratio, wide, carry_w, rate_tiles,
    xs, halo_s, halo_r, prod, gate, local, s_send, s_recv, t_send, t_recv, starts, e_send, e_recv, p_send, p_recv,
    gall, wg, acc, o_send,
    word_sem, in_sem, halo_sem, s_ssem, s_rsem, t_ssem, t_rsem, e_ssem, e_rsem, p_ssem, p_rsem,
    wx_sem, wf_rsem, wf_ssem, wb_rsem, wbz_ssem, wz_rsem, wz_ssem, wl_rsem, wr_rsem, wy_ssem, wh_rsem, wh_ssem, g_rsem, g_ssem, f_ssem, h_ssem, o_sem,
):
    chans, length = proj.shape[1], proj.shape[2]
    groups = chans // 128
    rows = w_shard.shape[0]
    half = w_shard.shape[1] // 2
    pieces = chans // KC
    steps = length // 8

    ctx = lax.axis_index("ctx")
    rep = lax.axis_index("rep")
    z = lax.rem(ctx, Z)
    y = lax.rem(ctx // Z, Y)
    xl = ctx // (Y * Z)
    xo = 1 - xl
    rep_core = rep + 1 - 2 * lax.rem(rep, 2)
    rep_far = rep + 2 - 4 * (rep // 2)

    def at(x_, y_, z_):
        return (x_ * Y + y_) * Z + z_

    def remote(src, dst, ssem, rsem, c, r=None):
        return pltpu.make_async_remote_copy(
            src_ref=src, dst_ref=dst, send_sem=ssem, recv_sem=rsem,
            device_id=(c, rep if r is None else r), device_id_type=pl.DeviceIdType.MESH,
        )

    nxt = lax.rem(ctx + 1, X * Y * Z)
    prv = lax.rem(ctx + X * Y * Z - 1, X * Y * Z)
    zr = at(xl, y, lax.rem(z + 1, Z))
    zl = at(xl, y, lax.rem(z + Z - 1, Z))

    bar = pltpu.get_barrier_semaphore()

    def hello(c, r):
        pl.semaphore_signal(bar, inc=1, device_id=(c, r), device_id_type=pl.DeviceIdType.MESH)

    ZH = Z // ZL
    zh = z // ZL
    plane = Y * ZL
    mine = y * ZL + lax.rem(z, ZL)

    def plane_peer(q):
        return at(xl, q // ZL, zh * ZL + lax.rem(q, ZL))

    def slab_peer(x_, h):
        return at(x_, y, h * ZL + lax.rem(z, ZL))

    up = at(xl, y, lax.rem(z + ZL, Z))
    down = at(xl, y, lax.rem(z + Z - ZL, Z))
    cx = at(xo, y, z)

    for c in (up, down, nxt, prv, zr, zl):
        hello(c, rep)

    @pl.loop(1, plane)
    def _(d):
        hello(plane_peer(lax.rem(mine + d, plane)), rep)

    hello(cx, rep)
    hello(ctx, rep_core)
    hello(cx, rep_far)
    reads = [
        pltpu.make_async_copy(proj_hbm.at[i], proj.at[i], in_sem.at[i]) for i in range(3)
    ]
    reads += [
        pltpu.make_async_copy(rates_hbm, rates, in_sem.at[3]),
        pltpu.make_async_copy(amps_hbm, amps, in_sem.at[4]),
        pltpu.make_async_copy(taps_hbm, taps, in_sem.at[5]),
    ]
    for read in reads:
        read.start()

    def lanes(g, width=128):
        return pl.ds(pl.multiple_of(g * width, width), width)

    eye = (
        lax.broadcasted_iota(jnp.int32, (length, length), 0)
        == lax.broadcasted_iota(jnp.int32, (length, length), 1)
    ).astype(BF16)

    for s in range(3):
        reads[s].wait()

        @pl.loop(0, groups)
        def _(g):
            xs[s, pl.ds(8, length), lanes(g)] = lax.dot_general(
                eye, proj[s, lanes(g), :], (((1,), (1,)), ((), ())), preferred_element_type=F32
            )

        xs[s, pl.ds(0, 8), :] = jnp.zeros((8, chans), F32)
    halo_s[...] = jnp.zeros_like(halo_s)
    for s in range(3):
        halo_s[pl.ds(2 * s, 2), :] = xs[s, pl.ds(8 + length - 2, 2), :]

    pl.semaphore_wait(bar, (plane - 1) + 7 + 2)

    def pass_on(i):
        for c in (up, down):
            pl.semaphore_signal(
                word_sem.at[i], inc=1, device_id=(c, rep), device_id_type=pl.DeviceIdType.MESH
            )

    pass_on(0)
    halo = remote(halo_s, halo_r, halo_sem.at[0], halo_sem.at[1], nxt)
    halo.start()

    RZ = Z // 2
    half_rows = rows // 2
    last = half // 4 if half >= 512 else half // 2
    lead, rest = pl.ds(0, half - last), pl.ds(half - last, last)

    def wcols(i):
        return w_shard.at[:, pl.ds(pl.multiple_of(i * half, half), half)]

    x_copy = remote(wcols(xo), wg.at[xl, y, z], wx_sem.at[0], wx_sem.at[1], cx)
    x_copy.start()
    own = pltpu.make_async_copy(wcols(xl), wg.at[xl, y, z], wx_sem.at[2])
    own.start()

    def y_of(d):
        return lax.rem(y + d, Y)

    def z_of(d):
        return lax.rem(z + d + Z, Z)

    y_next, y_prev = at(xl, y_of(1), z), at(xl, y_of(Y - 1), z)

    def w_half(d_y, d_z, i, ssem, rsem, c):
        part = wg.at[:, y_of(d_y), z_of(d_z), pl.ds(i * half_rows, half_rows), lead]
        return remote(part, part, ssem, rsem.at[i * Z + z_of(d_z)], c)

    def w_round(d_z, i, right, k):
        ssem = wz_ssem.at[(i * 2 + right) * RZ + k]
        return w_half(0, d_z, i, ssem, wz_rsem, zr if right else zl)

    def w_arrived(d_z, i):
        w_half(0, d_z, i, wx_sem.at[0], wz_rsem, ctx).wait_recv()

    def w_whole(d_y, d_z, ssem, rsem, c):
        part = wg.at[:, y_of(d_y), z_of(d_z), :, lead]
        return remote(part, part, ssem, rsem.at[z_of(d_z)], c)

    def w_spread(d_z):
        w_whole(0, d_z, wy_ssem.at[z_of(d_z)], wl_rsem, y_next).start()
        w_whole(0, d_z, wy_ssem.at[Z + z_of(d_z)], wr_rsem, y_prev).start()

    def w_relay(d_z):
        w_whole(Y - 1, d_z, wx_sem.at[0], wl_rsem, ctx).wait_recv()
        w_half(Y - 1, d_z, 0, wh_ssem.at[z_of(d_z)], wh_rsem, y_next).start()
        w_whole(1, d_z, wx_sem.at[0], wr_rsem, ctx).wait_recv()
        w_half(1, d_z, 1, wh_ssem.at[Z + z_of(d_z)], wh_rsem, y_prev).start()

    def w_relayed(d_z):
        for i in range(2):
            w_half(2, d_z, i, wx_sem.at[0], wh_rsem, ctx).wait_recv()

    def b_first(d_y, ssem, c):
        part = wg.at[:, y_of(d_y), z, :, rest]
        return remote(part, part, ssem, rsem=wf_rsem.at[y_of(d_y)], c=c)

    def b_copy(p, d_z, ssem, c):
        part = wg.at[:, pl.ds(p * (Y // 2), Y // 2), z_of(d_z), :, rest]
        return remote(part, part, ssem, rsem=wb_rsem.at[p * Z + z_of(d_z)], c=c)

    def b_round(p, d_z, right, k):
        return b_copy(p, d_z, wbz_ssem.at[(p * 2 + right) * RZ + k], zr if right else zl)

    def b_arrived(p, d_z):
        b_copy(p, d_z, wx_sem.at[0], ctx).wait_recv()

    def b_step(k):
        for j in range(1, Y if k == 0 else 1):
            b_first(j, wf_ssem.at[0], ctx).wait_recv()
        for p in range(2):
            if k > 0:
                b_arrived(p, -k)
            if k < RZ - 1 or p == 0:
                b_round(p, -k, 1, k).start()
            if k > 0:
                b_arrived(p, k)
            if k < RZ - 1 or p == 1:
                b_round(p, k, 0, k).start()

    def w_direct(d_z):
        for i in range(2):
            ssem = wh_ssem.at[i * Z + z_of(d_z)]
            w_half(0, d_z, i, ssem, wh_rsem, at(xl, y_of(2), z)).start()

    def w_sides(d_z):
        w_whole(Y - 1, d_z, wx_sem.at[0], wl_rsem, ctx).wait_recv()
        w_whole(1, d_z, wx_sem.at[0], wr_rsem, ctx).wait_recv()

    def w_start():
        own.wait()
        x_copy.wait_recv()
        for i in range(2):
            w_round(0, i, 1, 0).start()
            w_round(0, i, 0, 0).start()
        for j in range(1, Y):
            b_first(0, wf_ssem.at[j], at(xl, y_of(j), z)).start()
        w_spread(0)

    def w_step(k):
        if k >= RZ:
            return
        for i in range(2):
            w_arrived(-k, i)
            if k < RZ - 1 or i == 0:
                w_round(-k, i, 1, k).start()
            w_arrived(k, i)
            if k < RZ - 1 or i == 1:
                w_round(k, i, 0, k).start()
        b_step(k - 1)
        w_spread(-k)
        w_spread(k)
        if k > 1:
            w_relay(2 - k)
        if k > 2:
            w_relay(k - 2)

    def w_last():
        for i in range(2):
            w_arrived(RZ, i)
        w_direct(RZ)
        w_spread(RZ)
        b_step(RZ - 1)
        for k in (RZ - 2, RZ - 1):
            w_relay(-k)
            if k > 0:
                w_relay(k)

    sub = lax.broadcasted_iota(jnp.int32, (MODES, 8, 128), 1).astype(F32)
    for read in reads[3:]:
        read.wait()

    @pl.loop(0, groups)
    def _(g):
        r2 = rates[:, lanes(g)]
        w2 = amps[:, lanes(g)] * jnp.sqrt(2.0 * r2)
        rate_tiles[g] = r2[0:8]
        rate_tiles[groups + g] = r2[8:16]
        once = w2 * jnp.exp(-r2)
        carry_w[g] = once[0:8]
        carry_w[groups + g] = once[8:16]
        r = r2[:, None, :]
        ex[:, :, lanes(g)] = jnp.exp(-r * sub)
        back = jnp.exp(-r * (7.0 - sub))
        rev[:, :, lanes(g)] = back
        first[:, :, lanes(g)] = back * jnp.exp(-float(length - 8) * r)
        ratio[:, :, lanes(g)] = jnp.exp(-8.0 * r)
        wide[:, :, lanes(g)] = w2[:, None, :]

    w_start()

    def featured(g, begin, count):
        made = []
        for s in range(3):
            total = taps[s, pl.ds(0, 1), lanes(g)] * xs[s, pl.ds(8 + begin, count), lanes(g)]
            for j in range(1, 3):
                total = total + (
                    taps[s, pl.ds(j, 1), lanes(g)]
                    * xs[s, pl.ds(8 + begin - j, count), lanes(g)]
                )
            made.append(total)
        return made[0].astype(BF16).astype(F32), (made[1] * made[2]).astype(BF16).astype(F32)

    top = lax.broadcasted_iota(jnp.int32, (8, 128), 0) < 2

    @pl.loop(0, groups)
    def _(g):
        gate_here, prod_here = featured(g, 0, length)
        gate[:, lanes(g)] = gate_here
        prod[:, lanes(g)] = prod_here
        step = ratio[:, :, lanes(g)]
        state = jnp.where(top, 0.0, prod[pl.ds(0, 8), lanes(g)])[None] * step
        for a in range(1, steps):
            state = state + prod[pl.ds(8 * a, 8), lanes(g)][None]
            if a < steps - 1:
                state = state * step
        ends = jnp.sum(state * rev[:, :, lanes(g)], axis=1)
        s_send[g] = ends[0:8]
        s_send[groups + g] = ends[8:16]

    halo.wait_recv()
    keep = jnp.where(ctx > 0, 1.0, 0.0).astype(F32)
    for s in range(3):
        xs[s, pl.ds(6, 2), :] = halo_r[pl.ds(2 * s, 2), :] * keep

    @pl.loop(0, groups)
    def _(g):
        gate_here, prod_here = featured(g, 0, 8)
        gate[pl.ds(0, 8), lanes(g)] = gate_here
        prod[pl.ds(0, 8), lanes(g)] = prod_here
        more = jnp.sum(
            first[:, :, lanes(g)] * jnp.where(top, prod_here, 0.0)[None], axis=1
        )
        s_send[g] += more[0:8]
        s_send[groups + g] += more[8:16]

    pl.semaphore_wait(word_sem.at[0], 2)
    pass_on(1)
    s_recv[mine] = s_send[mine]

    @pl.loop(1, plane)
    def _(d):
        to = lax.rem(mine + d, plane)
        remote(
            s_send.at[to], s_recv.at[mine], s_ssem.at[d], s_rsem.at[mine], plane_peer(to)
        ).start()

    w_step(1)

    @pl.loop(0, groups)
    def _(g):
        q = wide[:, :, lanes(g)] * ex[:, :, lanes(g)]
        step = ratio[:, :, lanes(g)]
        for a in range(steps):
            local[pl.ds(8 * a, 8), lanes(g)] = jnp.sum(q, axis=0)
            q = q * step

    def dot(left, right):
        return jnp.dot(left, right, preferred_element_type=F32)

    @pl.loop(0, chans // 256)
    def _(g):
        h_hi, h_lo = split(local[:, lanes(g, 256)])
        h_spec = dot(fwd[...], jnp.concatenate([h_hi, h_hi], axis=0)) + dot(fwd[:, :length], h_lo)
        u = prod[:, lanes(g, 256)]
        u_hi = u.astype(BF16)
        u_spec = dot(fwd[...], jnp.concatenate([u_hi, u_hi], axis=0))
        u_re, u_im = u_spec[:length], u_spec[length:]
        h_re, h_im = h_spec[:length], h_spec[length:]
        joint = jnp.concatenate(
            [u_re * h_re - u_im * h_im, u_re * h_im + u_im * h_re], axis=0
        )
        j_hi, j_lo = split(joint)
        mixed = dot(bwd[...], j_hi)
        mixed = mixed[:length] + mixed[length:] + dot(bwd[:length, :], j_lo)
        local[:, lanes(g, 256)] = mixed + skip[:, lanes(g, 256)] * u

    w_step(2)

    @pl.loop(1, plane)
    def _(d):
        src = lax.rem(mine + d, plane)
        remote(s_send.at[mine], s_recv.at[src], s_ssem.at[d], s_rsem.at[src], ctx).wait_recv()

    tile_rate = rate_tiles[mine]
    block_decay = jnp.exp(-float(length) * tile_rate)
    for i in range(Y):
        total = jnp.zeros((8, 128), F32)
        for j in range(ZL):
            total = total * block_decay + s_recv[i * ZL + j]
        t_send[i] = total
        t_recv[zh, i] = total
    group = float(length * ZL)
    share = jnp.zeros((8, 128), F32)
    for i in range(Y):
        left = (Y * ZH - 1 - (i * ZH + zh)).astype(F32)
        share = share + t_send[i] * jnp.exp(-(group * left) * tile_rate)
    e_send[...] = share
    pl.semaphore_wait(word_sem.at[1], 2)

    for d in (2, 1, 3):
        to = lax.rem(zh + d, ZH)
        remote(t_send, t_recv.at[zh], t_ssem.at[d], t_rsem.at[zh], slab_peer(xl, to)).start()

    @pl.loop(0, ZH)
    def _(h):
        remote(e_send, e_recv.at[zh], e_ssem.at[h], e_rsem.at[zh], slab_peer(xo, h)).start()

    w_step(3)
    w_step(4)

    @pl.loop(1, ZH)
    def _(d):
        src = lax.rem(zh + d, ZH)
        remote(t_send, t_recv.at[src], t_ssem.at[d], t_rsem.at[src], ctx).wait_recv()

    @pl.loop(0, ZH)
    def _(h):
        remote(e_send, e_recv.at[h], e_ssem.at[h], e_rsem.at[h], ctx).wait_recv()

    group_decay = jnp.exp(-group * tile_rate)
    carry = jnp.zeros((8, 128), F32)
    for j in range(Y):
        for k in range(ZH):
            starts[j * ZH + k] = carry
            carry = carry * group_decay + t_recv[k, j]
    later = jnp.zeros((8, 128), F32)
    for k in range(ZH):
        later = later + e_recv[k]
    later = jnp.where(xl > 0, later, 0.0)
    for i in range(Y):
        n = i * ZH + zh
        carry = starts[n] + later * jnp.exp(-(group * n.astype(F32)) * tile_rate)
        for j in range(ZL):
            p_send[i * ZL + j] = carry
            carry = carry * block_decay + s_recv[i * ZL + j]
    p_recv[mine] = p_send[mine]

    @pl.loop(1, plane)
    def _(d):
        to = lax.rem(mine + d, plane)
        remote(
            p_send.at[to], p_recv.at[mine], p_ssem.at[d], p_rsem.at[mine], plane_peer(to)
        ).start()

    w_step(5)
    w_step(6)

    @pl.loop(1, plane)
    def _(d):
        src = lax.rem(mine + d, plane)
        remote(p_send.at[mine], p_recv.at[src], p_ssem.at[d], p_rsem.at[src], ctx).wait_recv()

    def piece(x_, r_, k):
        return gall.at[
            r_, pl.ds(pl.multiple_of(x_ * length, length), length), pl.ds(k * KC, KC)
        ]

    def g_copy(x_, r_, k, ssem, c, r):
        return remote(
            piece(x_, r_, k), piece(x_, r_, k), ssem, g_rsem.at[(x_ * REPS + r_) * pieces + k], c, r
        )

    def g_arrived(x_, r_, k):
        g_copy(x_, r_, k, g_ssem.at[0], ctx, rep).wait_recv()

    per = KC // 128

    def finish(k):
        for i in range(per):
            g = k * per + i
            before = jnp.concatenate(
                [p_recv[g] * carry_w[g], p_recv[groups + g] * carry_w[groups + g]], axis=0
            )
            q = before[:, None, :] * ex[:, :, lanes(g)]
            step = ratio[:, :, lanes(g)]
            for a in range(steps):
                here = (pl.ds(8 * a, 8), lanes(g))
                local[here] = local[here] + jnp.sum(q, axis=0)
                q = q * step
            long = local[:, lanes(g)].astype(BF16).astype(F32)
            here = pl.ds(pl.multiple_of(xl * length, length), length)
            gall[rep, here, lanes(g)] = (gate[:, lanes(g)] * long).astype(BF16)

    for k in range(pieces):
        finish(k)
        g_copy(xl, rep, k, g_ssem.at[3 * k], ctx, rep_core).start()
        g_copy(xl, rep, k, g_ssem.at[3 * k + 1], cx, rep).start()
        g_copy(xl, rep, k, g_ssem.at[3 * k + 2], cx, rep_far).start()

    def g_pass(k):
        g_arrived(xo, rep, k)
        if k % 2 == 0:
            g_copy(xo, rep, k, h_ssem.at[k], cx, rep_far).start()
        g_copy(xo, rep, k, f_ssem.at[3 * k], ctx, rep_core).start()
        g_arrived(xo, rep_far, k)
        if k % 2 == 1:
            g_copy(xo, rep_far, k, h_ssem.at[k], cx, rep).start()
        g_copy(xo, rep_far, k, f_ssem.at[3 * k + 1], ctx, rep_core).start()

    w_step(7)
    for k in range(pieces // 2):
        g_pass(k)
    w_last()
    for k in range(pieces // 2, pieces):
        g_pass(k)
    for p in range(2):
        b_arrived(p, RZ)
    w_sides(RZ)

    @pl.loop(0, Z)
    def _(d):
        w_relayed(d)

    def project(r_, here, cols=slice(None)):
        n = r_ * (chans // rows) // Z
        part = wg[n // Y, pl.ds(lax.rem(n, Y), chans // rows // Z), :, :, cols]
        part = part.reshape(chans, part.shape[-1])
        return jnp.dot(gall[r_, here, :], part, preferred_element_type=F32)

    both = pl.ds(0, X * length)
    acc[...] = project(rep, both)

    @pl.loop(0, pieces)
    def _(k):
        g_arrived(xl, rep_far, k)
        g_copy(xl, rep_far, k, f_ssem.at[3 * k + 2], ctx, rep_core).start()

    acc[...] += project(rep_far, both)
    core_far = rep_far + rep_core - rep

    @pl.loop(0, pieces)
    def _(k):
        for x_ in range(X):
            g_arrived(x_, rep_core, k)

    acc[...] += project(rep_core, both)

    @pl.loop(0, pieces)
    def _(k):
        for x_ in range(X):
            g_arrived(x_, core_far, k)

    def turn(x_, i, to):
        here = pl.ds(pl.multiple_of(x_ * length, length), length)
        cols = pl.ds(i * (half // 2), half // 2)
        done = acc[here, cols] + project(core_far, here, cols)
        to[cols, :] = done.T.astype(BF16)

    def swapped(i, x_, c):
        cols = pl.ds(i * (half // 2), half // 2)
        return remote(
            o_send.at[cols, :], out.at[x_, cols, :], o_sem.at[i], o_sem.at[2 + i], c
        )

    for i in range(2):
        turn(xo, i, o_send)
        swapped(i, xl, cx).start()
    for i in range(2):
        turn(xl, i, out.at[xl])

    halo.wait_send()
    x_copy.wait_send()

    @pl.loop(1, plane)
    def _(d):
        remote(s_send.at[0], s_recv.at[0], s_ssem.at[d], s_rsem.at[0], ctx).wait_send()
        remote(p_send.at[0], p_recv.at[0], p_ssem.at[d], p_rsem.at[0], ctx).wait_send()

    @pl.loop(1, ZH)
    def _(d):
        remote(t_send, t_recv.at[0], t_ssem.at[d], t_rsem.at[0], ctx).wait_send()

    @pl.loop(0, ZH)
    def _(h):
        remote(e_send, e_recv.at[0], e_ssem.at[h], e_rsem.at[0], ctx).wait_send()

    @pl.loop(0, Z)
    def _(i):
        for j in range(2):
            w_whole(0, 0, wy_ssem.at[j * Z + i], wl_rsem, ctx).wait_send()
            w_half(0, 0, 0, wh_ssem.at[j * Z + i], wh_rsem, ctx).wait_send()

    for j in range(1, Y):
        b_first(0, wf_ssem.at[j], ctx).wait_send()
    for k in range(RZ):
        for i in range(2):
            for right in range(2):
                if k < RZ - 1 or i != right:
                    w_round(0, i, right, k).wait_send()
                    b_round(i, 0, right, k).wait_send()

    @pl.loop(0, 3 * pieces)
    def _(i):
        g_copy(0, 0, 0, g_ssem.at[i], ctx, rep).wait_send()
        g_copy(0, 0, 0, f_ssem.at[i], ctx, rep).wait_send()

    @pl.loop(0, pieces)
    def _(i):
        g_copy(0, 0, 0, h_ssem.at[i], ctx, rep).wait_send()

    for i in range(2):
        swapped(i, xl, cx).wait_send()
        swapped(i, xo, ctx).wait_recv()


def per_device(projected, short_taps, residues, decay_rates, skip_gain, out_weight):
    _, chans, length = projected.shape
    groups = chans // 128
    rows, feats = out_weight.shape
    half = feats // X
    pieces = chans // KC
    fwd, bwd = tables(length)
    vm = pltpu.VMEM
    dma = pltpu.SemaphoreType.DMA
    out = pl.pallas_call(
        kernel,
        out_shape=pltpu.VMEM((X, half, length), BF16),
        in_specs=[pl.BlockSpec(memory_space=pltpu.HBM)] * 4
        + [pl.BlockSpec(memory_space=vm)] * 3
        + [pl.BlockSpec(memory_space=pltpu.HBM)],
        out_specs=pl.BlockSpec(memory_space=vm),
        scratch_shapes=[
            vm((3, chans, length), BF16),
            vm((3, 3, chans), F32),
            vm((MODES, chans), F32),
            vm((MODES, chans), F32),
            vm((MODES, 8, chans), F32),
            vm((MODES, 8, chans), F32),
            vm((MODES, 8, chans), F32),
            vm((MODES, 1, chans), F32),
            vm((MODES, 1, chans), F32),
            vm((Y * ZL, 8, 128), F32),
            vm((Y * ZL, 8, 128), F32),
            vm((3, length + 8, chans), F32),
            vm((8, chans), F32),
            vm((8, chans), F32),
            vm((length, chans), F32),
            vm((length, chans), F32),
            vm((length, chans), F32),
            vm((Y * ZL, 8, 128), F32),
            vm((Y * ZL, 8, 128), F32),
            vm((Y, 8, 128), F32),
            vm((Z // ZL, Y, 8, 128), F32),
            vm((Y * Z // ZL, 8, 128), F32),
            vm((8, 128), F32),
            vm((Z // ZL, 8, 128), F32),
            vm((Y * ZL, 8, 128), F32),
            vm((Y * ZL, 8, 128), F32),
            vm((REPS, X * length, chans), BF16),
            vm((X, Y, Z, rows, half), BF16),
            vm((X * length, half), F32),
            vm((half, length), BF16),
            pltpu.SemaphoreType.REGULAR((2,)),
            dma((6,)),
            dma((2,)),
            dma((Y * ZL,)),
            dma((Y * ZL,)),
            dma((Z // ZL,)),
            dma((Z // ZL,)),
            dma((Z // ZL,)),
            dma((Z // ZL,)),
            dma((Y * ZL,)),
            dma((Y * ZL,)),
            dma((3,)),
            dma((Y,)),
            dma((Y,)),
            dma((2 * Z,)),
            dma((2 * Z,)),
            dma((2 * Z,)),
            dma((2 * Z,)),
            dma((Z,)),
            dma((Z,)),
            dma((2 * Z,)),
            dma((2 * Z,)),
            dma((2 * Z,)),
            dma((X * REPS * pieces,)),
            dma((3 * pieces,)),
            dma((3 * pieces,)),
            dma((pieces,)),
            dma((4,)),
        ],
        compiler_params=pltpu.CompilerParams(
            collective_id=0, has_side_effects=True, vmem_limit_bytes=60 * 1024 * 1024
        ),
        name="hyena",
    )(
        projected, short_taps.transpose(0, 2, 1), residues.T, decay_rates.T, skip_gain[None],
        jnp.asarray(fwd), jnp.asarray(bwd), out_weight,
    )
    return out.reshape(feats, length)


def solution(mesh):
    in_specs = (
        P(None, "rep", "ctx"),
        P(None, "rep", None),
        P("rep", None),
        P("rep", None),
        P("rep"),
        P("ctx", "rep"),
    )
    out_specs = P("rep", "ctx")
    return jax.shard_map(
        per_device, mesh=mesh, in_specs=in_specs, out_specs=out_specs, check_vma=False
    )
```
